256 devices in a mesh: tm: 8 (over x, core), height: 4 (over y), dp: 8 (over z).
Axes of the slice: x: 4, y: 4, z: 8, core: 2. Of those that a mesh axis runs over, the one named last changes fastest.
Arguments:
- activations: bfloat16 [8, 16, 4, 256, 256], P('dp', 'tm', 'height'), may hold values from -9 to 9
- cotangent: bfloat16 [8, 16, 4, 256, 256], P('dp', 'tm', 'height'), may hold values from -9 to 9
- clip_frames: int32 [8], P('dp'), may hold values from 15 to 16, as said below
- conv_weight: bfloat16 [256, 27, 256], P('dp'), may hold values from -0.078125 to 0.078125
- group_centre: float32 [8, 32], P('dp'), may hold values from -3 to 3
- group_scale: float32 [8, 32], P('dp'), may hold values from 0.5 to 2
- norm_gain: float32 [256], replicated, may hold values from 0.5 to 1.5
- norm_bias: float32 [256], replicated, may hold values from -0.5 to 0.5
Outputs:
- grad_input: bfloat16 [8, 16, 4, 256, 256], P('dp', 'tm', 'height')
- weight_grad: bfloat16 [6912, 256], P(('tm', 'height', 'dp'))
The draws below stay inside these ranges and needn't reach their ends.
Inputs may be any that keep to these rules, and one draw needn't show every extreme that they name: `clip_frames`: some clip has exactly 16 frames and another exactly 15 in every draw.
All inputs are finite; a program needn't handle non-finite values.
Results may differ from the reference program's by a relative error of at most 0.0031.
Values may be sent and summed in bfloat16 or wider, within the bound.
A program may use at most 64 MiB of HBM per device.

```python
import math
import jax
import jax.numpy as jnp
from jax import lax

CH = 256
GROUPS = 32
TAPS = 27
COLS = 256
T_DEV = 2
CLIPS = 8
FRAMES = 16
HROWS = 4


def ramped_field(key, salt):
    base = jax.random.fold_in(key, salt)
    key_noise, key_sign = jax.random.split(base, 2)
    shape = (CLIPS, FRAMES, HROWS, COLS, CH)
    frame_pos = jnp.arange(FRAMES, dtype=jnp.float32)[None, :, None, None, None] / FRAMES
    row_pos = jnp.arange(HROWS, dtype=jnp.float32)[None, None, :, None, None] / HROWS
    level = 0.5 + 0.5 * (frame_pos + row_pos)
    signs = jnp.where(jax.random.bernoulli(key_sign, 0.5, (CLIPS, 1, 1, 1, CH)), 1.0, -1.0)
    noise = jnp.clip(jax.random.normal(key_noise, shape, jnp.float32), -4.0, 4.0)
    return noise + signs * level


def draw_activations(key, part):
    return ramped_field(key, 11).astype(jnp.bfloat16)


def draw_cotangent(key, part):
    return ramped_field(key, 23).astype(jnp.bfloat16)


def draw_clip_frames(key, part):
    key_len, key_full, key_short = jax.random.split(jax.random.fold_in(key, 37), 3)
    lengths = FRAMES - jax.random.randint(key_len, (CLIPS,), 0, T_DEV)
    full_at = jax.random.randint(key_full, (), 0, CLIPS)
    short_at = (full_at + 1 + jax.random.randint(key_short, (), 0, CLIPS - 1)) % CLIPS
    position = jnp.arange(CLIPS)
    lengths = jnp.where(position == full_at, FRAMES, lengths)
    lengths = jnp.where(position == short_at, FRAMES - T_DEV + 1, lengths)
    return lengths.astype(jnp.int32)


def level_of(rng, shape, cuts, least, top_value):
    gain, own = 1.0, jax.random.fold_in(rng, 6)
    for axis_at, parts in cuts:
        steps = jnp.exp(jax.random.uniform(jax.random.fold_in(own, axis_at), (parts,), jnp.float32, least / len(cuts), top_value / len(cuts)))
        gain = gain * jnp.repeat(steps, shape[axis_at] // parts).reshape([-1 if axis == axis_at else 1 for axis in range(len(shape))])
    return gain


def scatter_about(key, shape, width, bound, cuts=(), kind=jnp.bfloat16):
    values = width * jax.random.normal(key, shape, jnp.float32)
    if cuts:
        values = values * level_of(key, shape, cuts, -0.22, 0.18)
    return jnp.clip(values, -bound, bound).astype(kind)


def setup_inputs(seed: int = 0) -> dict:
    key_of = jax.random.split(jax.random.key(seed), 9)
    return {
        "activations": draw_activations(jax.random.fold_in(key_of[8], 71), 0),
        "cotangent": draw_cotangent(jax.random.fold_in(key_of[8], 71), 0),
        "clip_frames": draw_clip_frames(jax.random.fold_in(key_of[8], 71), 0),
        "conv_weight": scatter_about(key_of[3], (CH, TAPS, CH), (TAPS * CH) ** -0.5, 0.078125, ((0, 8),)),
        "group_centre": scatter_about(key_of[4], (CLIPS, GROUPS), 0.3, 3.0, ((0, 8),), jnp.float32),
        "group_scale": jnp.clip(jnp.exp(math.log(2.0) - 1.3862944 * jax.random.uniform(key_of[5], (CLIPS, GROUPS), jnp.float32) ** level_of(key_of[5], (CLIPS, GROUPS), ((0, 8),), -0.2, 0.2)), 0.5, 2.0),
        "norm_gain": jnp.clip(1.0 + 0.1 * jax.random.normal(key_of[6], (CH,), jnp.float32), 0.5, 1.5),
        "norm_bias": jnp.clip(jax.random.uniform(key_of[7], (CH,), jnp.float32, -0.5, 0.5), -0.5, 0.5),
    }


def contract_inner(matrix, operand):
    return lax.dot_general(matrix, operand, (((1,), (1,)), ((), ())), preferred_element_type=jnp.float32)


def contract_rows(matrix, operand):
    return lax.dot_general(matrix, operand, (((0,), (0,)), ((), ())), preferred_element_type=jnp.float32)


def reference(activations, cotangent, clip_frames, conv_weight, group_centre, group_scale, norm_gain, norm_bias):
    per_group = CH // GROUPS

    def one_clip(inputs):
        clip_acts, clip_cot, clip_len, centre, spread = inputs
        validity = (jnp.arange(FRAMES) < clip_len).astype(jnp.float32)[:, None, None, None]
        grouped = clip_acts.astype(jnp.float32).reshape(FRAMES, HROWS, COLS, GROUPS, per_group)
        normed = ((grouped - centre[:, None]) * spread[:, None]).reshape(FRAMES, HROWS, COLS, CH)
        shifted = normed * norm_gain + norm_bias
        sigmoid_val = jax.nn.sigmoid(shifted)
        conv_input = (shifted * sigmoid_val * validity).astype(jnp.bfloat16)
        masked = clip_cot * validity.astype(jnp.bfloat16)
        padded = jnp.pad(masked, ((0, 2), (1, 1), (1, 1), (0, 0)))
        flat_input = conv_input.reshape(-1, CH)
        input_grad = jnp.zeros((FRAMES * HROWS * COLS, CH), jnp.float32)
        per_tap = []
        for tap_idx in range(TAPS):
            tap_t, tap_h, tap_w = tap_idx // 9, (tap_idx // 3) % 3, tap_idx % 3
            window = padded[2 - tap_t:2 - tap_t + FRAMES, 2 - tap_h:2 - tap_h + HROWS, 2 - tap_w:2 - tap_w + COLS].reshape(-1, CH)
            input_grad = input_grad + contract_inner(window, conv_weight[:, tap_idx, :])
            per_tap.append(contract_rows(flat_input, window))
        weight_part = jnp.stack(per_tap, axis=1)
        derivative = sigmoid_val * (1.0 + shifted * (1.0 - sigmoid_val))
        upstream = input_grad.reshape(FRAMES, HROWS, COLS, CH) * derivative * validity * norm_gain
        up_grouped = upstream.reshape(-1, GROUPS, per_group)
        normed_grouped = normed.reshape(-1, GROUPS, per_group)
        first_sum = jnp.sum(up_grouped, axis=(0, 2))
        second_sum = jnp.sum(up_grouped * normed_grouped, axis=(0, 2))
        population = clip_len.astype(jnp.float32) * (HROWS * COLS * per_group)
        correction = (first_sum / population)[:, None] + normed_grouped * (second_sum / population)[:, None]
        grad_flat = spread[:, None] * (up_grouped - correction)
        grad_clip = grad_flat.reshape(FRAMES, HROWS, COLS, CH) * validity
        return grad_clip.astype(jnp.bfloat16), weight_part

    grad_out, clip_parts = lax.map(one_clip, (activations, cotangent, clip_frames, group_centre, group_scale))
    summed = jnp.sum(clip_parts, axis=0) / (CLIPS * FRAMES * HROWS * COLS)
    return grad_out, summed.reshape(CH * TAPS, CH).astype(jnp.bfloat16)
```

```python
import functools

import jax
import jax.numpy as jnp
from jax import lax
from jax.experimental import pallas as pl
from jax.experimental.pallas import tpu as pltpu
from jax.sharding import PartitionSpec as P

CORES = 2
PER = 2
MESH = pl.DeviceIdType.MESH
F32 = jnp.float32
BF16 = jnp.bfloat16


def nt(a, b):
    return lax.dot_general(a, b, (((1,), (1,)), ((), ())), preferred_element_type=F32)


def nn(a, b):
    return lax.dot_general(a, b, (((1,), (0,)), ((), ())), preferred_element_type=F32)


def tn(a, b):
    return lax.dot_general(a, b, (((0,), (0,)), ((), ())), preferred_element_type=F32)


def fused(
    X, Y, Z,
    clip_frames, acts, cot, weight, centre, spread, gain, bias,
    out, wout,
    act_in, act_send, act_all, cots, w_all, w_rows, w_taps, lhs, grad, normed, slope,
    total, x_send, x_recv, row_sum, z_send, z_recv, s_send, s_recv, g_send, g_recv,
    act_sem, cot_sem, own_send, fwd_send, sis_send, halo_send, a_snd, a_rcv, w_snd, w_rcv,
    x_snd, x_rcv, z_snd, z_rcv, s_snd, s_rcv, g_snd, g_rcv,
):
    tm = lax.axis_index("tm")
    y = lax.axis_index("height")
    z = lax.axis_index("dp")
    x = tm // CORES
    c = tm % CORES
    span = CORES * PER
    cols, ch = cots.shape[2], cots.shape[3]
    chunk = act_all.shape[2]
    lead = 2
    halves = ch // 128

    def dev(xx, cc, yy, zz):
        return (xx * CORES + cc, yy, zz)

    def remote(src, dst, snd, rcv, target):
        return pltpu.make_async_remote_copy(
            src_ref=src, dst_ref=dst, send_sem=snd, recv_sem=rcv,
            device_id=target, device_id_type=MESH,
        )

    up, down = (y + 1) % Y, (y + Y - 1) % Y
    prev_x, next_x = (x + X - 1) % X, (x + 1) % X
    sister = dev(x, 1 - c, y, z)

    act_copy = pltpu.make_async_copy(acts, act_in, act_sem)
    act_copy.start()
    for k in range(PER):
        pltpu.make_async_copy(cot.at[k], cots.at[PER * c + k, y], cot_sem.at[PER * c + k, y]).start()

    barrier = pltpu.get_barrier_semaphore()
    partners = [
        dev(x, (c + dc) % CORES, (y + dy) % Y, z)
        for dc in range(CORES) for dy in range(Y) if dc or dy
    ]
    partners += [dev((x + dx) % X, c, y, z) for dx in range(1, X)]
    partners += [dev(x, c, y, (z + dz) % Z) for dz in range(1, Z)]
    for target in partners:
        pl.semaphore_signal(barrier, inc=1, device_id=target, device_id_type=MESH)

    @pl.when(c == 0)
    def _():
        pl.semaphore_signal(barrier, inc=1, device_id=dev(prev_x, 1, y, z), device_id_type=MESH)

    @pl.when(c == 1)
    def _():
        pl.semaphore_signal(barrier, inc=1, device_id=dev(next_x, 0, y, z), device_id_type=MESH)

    pl.semaphore_wait(barrier, len(partners) + 1)

    def cot_to(k, row, target, snd):
        src = cot.at[k] if row is None else cots.at[PER * c + k, row]
        at = y if row is None else row
        return remote(src, cots.at[PER * c + k, at], snd, cot_sem.at[PER * c + k, at], target)

    def halo_to(k, row, slot):
        src = cot.at[k] if row is None else cots.at[PER * c + k, row]
        at = y if row is None else row
        return remote(
            src, cots.at[span + k, at], halo_send.at[k, slot], cot_sem.at[span + k, at],
            dev(prev_x, k, y, z),
        )

    sends = []

    def go(copy):
        copy.start()
        sends.append(copy)

    for k in range(PER):
        ends = (up, down) if k == 0 else (down, up)
        for n, row in enumerate(ends):
            go(cot_to(k, None, dev(x, c, row, z), own_send.at[k, n]))
    for k in range(PER):
        go(cot_to(k, None, sister, sis_send.at[k, 0]))

        @pl.when(c == 0)
        def _():
            halo_to(k, None, 0).start()

    mine = (z % CORES) == c
    wsrc = weight.at[pl.ds(y * Z, Z)]

    @pl.when(mine)
    def _():
        pltpu.make_async_copy(wsrc, w_all.at[z // CORES], w_rcv.at[z // CORES]).start()
        for d in range(1, Z):
            remote(
                wsrc, w_all.at[z // CORES], w_snd.at[d - 1], w_rcv.at[z // CORES],
                dev(x, c, y, (z + d) % Z),
            ).start()

    row_id = lax.broadcasted_iota(jnp.int32, (ch, ch), 0)
    col_id = lax.broadcasted_iota(jnp.int32, (ch, ch), 1)
    half = ch // X
    per_core = half // CORES
    order = (
        ((row_id // Z) % X) * half + (row_id // (chunk * Y)) * per_core
        + ((row_id // chunk) % Y) * Z + row_id % Z
    )
    pick = jnp.where(order == col_id, 1.0, 0.0).astype(BF16)
    act_copy.wait()
    for k in range(PER):
        act_send[:, k] = nt(pick, act_in[k]).astype(BF16).reshape(CORES * Y, chunk, cols)
    around = [(dc, dy) for dc in range(CORES) for dy in range(Y) if dc or dy]
    for n, (dc, dy) in enumerate(around):
        cc, yy = (c + dc) % CORES, (y + dy) % Y
        go(remote(
            act_send.at[cc * Y + yy], act_all.at[pl.ds(PER * c, PER), y], a_snd.at[n], a_rcv.at[n],
            dev(x, cc, yy, z),
        ))
    act_all[pl.ds(PER * c, PER), y] = act_send[c * Y + y]

    def clear(s, _):
        grad[s] = jnp.zeros(grad.shape[1:], F32)
        for edge in (0, Y + 1):
            lhs[s, edge] = jnp.zeros(lhs.shape[2:], BF16)
        return 0

    lax.fori_loop(0, span, clear, 0)
    total[...] = jnp.zeros(total.shape, F32)

    def arrived(f, row):
        remote(
            cots.at[f, row], cots.at[f, row], own_send.at[0, 0], cot_sem.at[f, row], sister
        ).wait_recv()

    across = (y + 2) % Y
    steps = [(0, down, up), (1, up, down), (0, up, None), (1, down, None), (0, across, None), (1, across, None)]
    arrived_own = []
    seen = [1, 1]
    for k, row, on in steps:
        arrived(PER * c + k, row)
        if on is not None:
            go(cot_to(k, row, dev(x, c, on, z), fwd_send.at[k]))
        n = seen[k]
        seen[k] += 1
        go(cot_to(k, row, sister, sis_send.at[k, n]))

        @pl.when(c == 0)
        def _():
            halo_to(k, row, n).start()

    for k in range(PER):
        pltpu.make_async_copy(cot.at[k], cots.at[PER * c + k, y], cot_sem.at[PER * c + k, y]).wait()

    for n, (dc, dy) in enumerate(around):
        cs, ys = (c + dc) % CORES, (y + Y - dy) % Y
        remote(
            act_send.at[0], act_all.at[pl.ds(PER * cs, PER), ys], a_snd.at[n], a_rcv.at[n], sister
        ).wait_recv()

    i = lax.broadcasted_iota(jnp.int32, (chunk, 1), 0)
    channel = (i // Z) * half + c * per_core + y * Z + i % Z
    groups = centre.shape[1]
    group = (i // Z) * (groups // X) + c * (groups // X // CORES) + y

    def column(row, index):
        lane = lax.broadcasted_iota(jnp.int32, (chunk, row.shape[1]), 1)
        return jnp.sum(jnp.where(lane == index, row, 0.0), axis=1, keepdims=True)

    mean, scale = column(centre[...], group), column(spread[...], group)
    gains, biases = column(gain[...], channel), column(bias[...], channel)
    clip_len = clip_frames[0]

    def valid(f):
        return jnp.where(x * span + f < clip_len, 1.0, 0.0).astype(F32)

    lane = lax.broadcasted_iota(jnp.int32, (chunk, cols), 1)

    def prepare(t, _):
        s, r = t // Y, t % Y
        v = valid(s)
        norm = (act_all[s, r].astype(F32) - mean) * scale
        shifted = norm * gains + biases
        sig = jax.nn.sigmoid(shifted)
        normed[s, r] = norm
        slope[s, r] = sig * (1.0 + shifted * (1.0 - sig)) * v * gains
        a = shifted * sig * v
        lhs[s, r + 1, pl.ds(0, chunk)] = jnp.where(lane == 0, 0.0, pltpu.roll(a, 1, 1)).astype(BF16)
        lhs[s, r + 1, pl.ds(chunk, chunk)] = a.astype(BF16)
        lhs[s, r + 1, pl.ds(2 * chunk, chunk)] = jnp.where(
            lane == cols - 1, 0.0, pltpu.roll(a, cols - 1, 1)
        ).astype(BF16)
        return 0

    lax.fori_loop(0, span * Y, prepare, 0)

    rows3 = lhs.shape[2]

    def taps_of(f):
        return max(0, lead - f), min(3, span + lead - f)

    def masked(f, r):
        return jnp.where(x * span + f < clip_len, cots[f, r], jnp.zeros((cols, ch), BF16))

    def weight_term(f):
        k0, k1 = taps_of(f)
        s0, n = f - lead + k0, k1 - k0

        def body(r, _):
            left = lhs[pl.ds(s0, n), pl.ds(r, 3)].reshape(n * 3 * rows3, cols)
            total[pl.ds(k0, n)] += nn(left, masked(f, r)).reshape(n, 9, chunk, ch)
            return 0

        lax.fori_loop(0, Y, body, 0)

    tap_rows = 9 * Z

    def reduce_x(kt):
        for xx in range(X):
            x_send[kt, xx, pl.ds(0, tap_rows)] = (
                total[kt, :, pl.ds(xx * Z, Z)].reshape(tap_rows, ch).astype(BF16)
            )
            x_send[kt, xx, pl.ds(tap_rows, x_send.shape[2] - tap_rows)] = jnp.zeros(
                (x_send.shape[2] - tap_rows, ch), BF16
            )
        for d in range(1, X):
            xx = (x + d) % X
            go(remote(
                x_send.at[kt, xx], x_recv.at[kt, d - 1], x_snd.at[kt, d - 1], x_rcv.at[kt, d - 1],
                dev(xx, c, y, z),
            ))

    for f in range(span):
        @pl.when(c != f // PER)
        def _():
            for r in range(Y):
                arrived(f, r)

        weight_term(f)
    reduce_x(2)

    def halo_on(r, n):
        return remote(
            cots.at[span + c, r], cots.at[span + c, r], sis_send.at[n, Y], cot_sem.at[span + c, r], sister
        )

    for d in range(Y):
        r = (y + d) % Y
        arrived(span + c, r)
        copy = remote(
            cots.at[span + c, r], cots.at[span + c, r], fwd_send.at[PER + d], cot_sem.at[span + c, r], sister
        )
        go(copy)
    for f in range(span, span + lead):
        @pl.when(c != f - span)
        def _():
            for r in range(Y):
                arrived(f, r)

        weight_term(f)
        reduce_x(span + 1 - f)

    for n in range(X):
        pltpu.make_async_copy(w_all.at[n], w_all.at[n], w_rcv.at[n]).wait()

    def by_tap(i, _):
        rows = w_all[i // Z, i % Z].astype(F32)
        for h in range(halves):
            w_rows[h, pl.ds(i, 27, chunk), :] = rows[:, h * 128 : (h + 1) * 128]
        return 0

    lax.fori_loop(0, chunk, by_tap, 0)
    for h in range(halves):
        w_taps[:, :, :, pl.ds(h * 128, 128)] = w_rows[h].astype(BF16).reshape(w_taps.shape[:3] + (128,))

    def input_term(f):
        k0, k1 = taps_of(f)
        s0, n = f - lead + k0, k1 - k0

        def body(r, _):
            left = w_taps[pl.ds(k0, n)].reshape(n * 3 * rows3, ch)
            part = nt(left, masked(f, r)).reshape(n, 3, rows3, cols)
            grad[pl.ds(s0, n), pl.ds(r, 3)] += part
            return 0

        lax.fori_loop(0, Y, body, 0)

    for f in range(span + lead):
        input_term(f)

    def gather(t, carry):
        first, second = carry
        s, r = t // Y, t % Y
        g0 = grad[s, r + 1, pl.ds(0, chunk)]
        g1 = grad[s, r + 1, pl.ds(chunk, chunk)]
        g2 = grad[s, r + 1, pl.ds(2 * chunk, chunk)]
        whole = (
            jnp.where(lane == cols - 1, 0.0, pltpu.roll(g0, cols - 1, 1)) + g1
            + jnp.where(lane == 0, 0.0, pltpu.roll(g2, 1, 1))
        )
        upstream = whole * slope[s, r]
        slope[s, r] = upstream
        return first + upstream, second + upstream * normed[s, r]

    nothing = jnp.zeros((chunk, cols), F32)
    first, second = lax.fori_loop(0, span * Y, gather, (nothing, nothing))
    slim = lax.broadcasted_iota(jnp.int32, (chunk, 128), 1)
    first = jnp.sum(first, axis=1, keepdims=True)
    second = jnp.sum(second, axis=1, keepdims=True)
    s_send[...] = jnp.where(slim == 0, first, jnp.where(slim == 1, second, 0.0))
    for d in range(1, X):
        go(remote(
            s_send, s_recv.at[d - 1], s_snd.at[d - 1], s_rcv.at[d - 1], dev((x + d) % X, c, y, z)
        ))

    for kt in (2, 1, 0):
        for d in range(1, X):
            pltpu.make_async_copy(x_recv.at[kt, d - 1], x_recv.at[kt, d - 1], x_rcv.at[kt, d - 1]).wait()
        part = total[kt, :, pl.ds(x * Z, Z)].reshape(tap_rows, ch)
        for d in range(1, X):
            part = part + x_recv[kt, d - 1, pl.ds(0, tap_rows)].astype(F32)
        for h in range(halves):
            row_sum[h, pl.ds(kt * tap_rows, tap_rows)] = part[:, h * 128 : (h + 1) * 128]
    for zz in range(Z):
        for h in range(halves):
            z_send[zz, :, pl.ds(h * 128, 128)] = row_sum[h, pl.ds(zz, 27, Z), :]
    for d in range(1, Z):
        zz = (z + d) % Z
        go(remote(z_send.at[zz], z_recv.at[d - 1], z_snd.at[d - 1], z_rcv.at[d - 1], dev(x, c, y, zz)))

    for d in range(1, X):
        pltpu.make_async_copy(s_recv.at[d - 1], s_recv.at[d - 1], s_rcv.at[d - 1]).wait()
    both = s_send[...]
    for d in range(1, X):
        both = both + s_recv[d - 1]
    both = both.reshape(X, Z, 128)
    both = jnp.broadcast_to(jnp.sum(both, axis=1, keepdims=True), (X, Z, 128)).reshape(chunk, 128)
    population = clip_len.astype(F32) * (Y * cols * Z)
    first = jnp.sum(jnp.where(slim == 0, both, 0.0), axis=1, keepdims=True) / population
    second = jnp.sum(jnp.where(slim == 1, both, 0.0), axis=1, keepdims=True) / population

    def finish(t, _):
        s, r = t // Y, t % Y
        value = scale * (slope[s, r] - first - normed[s, r] * second) * valid(s)
        g_send[s, r] = value.astype(BF16)
        return 0

    lax.fori_loop(0, span * Y, finish, 0)
    for n, (dc, dy) in enumerate(around):
        cc, yy = (c + dc) % CORES, (y + dy) % Y
        go(remote(
            g_send.at[pl.ds(PER * cc, PER), yy], g_recv.at[c * Y + y], g_snd.at[n], g_rcv.at[n],
            dev(x, cc, yy, z),
        ))
    g_recv[c * Y + y] = g_send[pl.ds(PER * c, PER), y]

    for d in range(1, Z):
        pltpu.make_async_copy(z_recv.at[d - 1], z_recv.at[d - 1], z_rcv.at[d - 1]).wait()
    final = z_send[z]
    for d in range(1, Z):
        final = final + z_recv[d - 1]
    cells = X * Y * Z * CORES * PER * cols
    wout[...] = (final * (1.0 / cells)).astype(BF16)

    for n, (dc, dy) in enumerate(around):
        cs, ys = (c + dc) % CORES, (y + Y - dy) % Y
        remote(
            g_send.at[pl.ds(0, PER), 0], g_recv.at[cs * Y + ys], g_snd.at[n], g_rcv.at[n], sister
        ).wait_recv()
    for k in range(PER):
        out[k] = tn(g_recv[:, k].reshape(ch, cols), pick).astype(BF16)

    for copy in sends:
        copy.wait_send()

    @pl.when(c == 0)
    def _():
        for k in range(PER):
            for n in range(Y):
                halo_to(k, y, n).wait_send()

    @pl.when(mine)
    def _():
        for d in range(1, Z):
            remote(
                wsrc, w_all.at[z // CORES], w_snd.at[d - 1], w_rcv.at[z // CORES], sister
            ).wait_send()


def per_device(X, Y, Z, acts, cot, clip_frames, weight, centre, spread, gain, bias):
    _, per, _, cols, ch = acts.shape
    span, lead = CORES * per, 2
    chunk = ch // (CORES * Y)
    taps = weight.shape[1]
    dma = pltpu.SemaphoreType.DMA
    hbm = pl.BlockSpec(memory_space=pl.ANY)
    vmem = pl.BlockSpec(memory_space=pltpu.VMEM)
    tap_rows = -(-9 * Z // 16) * 16
    grad_input, weight_grad = pl.pallas_call(
        functools.partial(fused, X, Y, Z),
        out_shape=(
            jax.ShapeDtypeStruct((per, cols, ch), BF16),
            jax.ShapeDtypeStruct((taps, ch), BF16),
        ),
        in_specs=[pl.BlockSpec(memory_space=pltpu.SMEM), hbm, hbm, hbm, vmem, vmem, vmem, vmem],
        out_specs=(vmem, vmem),
        scratch_shapes=[
            pltpu.VMEM((per, cols, ch), BF16),
            pltpu.VMEM((CORES * Y, per, chunk, cols), BF16),
            pltpu.VMEM((span, Y, chunk, cols), BF16),
            pltpu.VMEM((span + lead, Y, cols, ch), BF16),
            pltpu.VMEM((X, Z, taps, ch), BF16),
            pltpu.VMEM((ch // 128, taps * chunk, 128), F32),
            pltpu.VMEM((3, 3, 3 * chunk, ch), BF16),
            pltpu.VMEM((span, Y + 2, 3 * chunk, cols), BF16),
            pltpu.VMEM((span, Y + 2, 3 * chunk, cols), F32),
            pltpu.VMEM((span, Y, chunk, cols), F32),
            pltpu.VMEM((span, Y, chunk, cols), F32),
            pltpu.VMEM((3, 9, chunk, ch), F32),
            pltpu.VMEM((3, X, tap_rows, ch), BF16),
            pltpu.VMEM((3, X - 1, tap_rows, ch), BF16),
            pltpu.VMEM((ch // 128, taps * Z, 128), F32),
            pltpu.VMEM((Z, taps, ch), F32),
            pltpu.VMEM((Z - 1, taps, ch), F32),
            pltpu.VMEM((chunk, 128), F32),
            pltpu.VMEM((X - 1, chunk, 128), F32),
            pltpu.VMEM((span, Y, chunk, cols), BF16),
            pltpu.VMEM((CORES * Y, per, chunk, cols), BF16),
            dma,
            dma((span + lead, Y)),
            dma((per, 2)),
            dma((per + Y,)),
            dma((per, Y)),
            dma((per, Y)),
            dma((CORES * Y - 1,)),
            dma((CORES * Y - 1,)),
            dma((Z - 1,)),
            dma((X,)),
            dma((3, X - 1)),
            dma((3, X - 1)),
            dma((Z - 1,)),
            dma((Z - 1,)),
            dma((X - 1,)),
            dma((X - 1,)),
            dma((CORES * Y - 1,)),
            dma((CORES * Y - 1,)),
        ],
        compiler_params=pltpu.CompilerParams(
            collective_id=0, has_side_effects=True, vmem_limit_bytes=48 * 1024 * 1024
        ),
    )(
        clip_frames,
        acts.reshape(per, cols, ch),
        cot.reshape(per, cols, ch),
        weight,
        centre,
        spread,
        gain.reshape(1, ch),
        bias.reshape(1, ch),
    )
    return grad_input.reshape(1, per, 1, cols, ch), weight_grad


def solution(mesh):
    X, Y, Z = mesh.shape["tm"] // CORES, mesh.shape["height"], mesh.shape["dp"]
    return jax.shard_map(
        functools.partial(per_device, X, Y, Z),
        mesh=mesh,
        in_specs=(
            P("dp", "tm", "height", None, None),
            P("dp", "tm", "height", None, None),
            P("dp"),
            P("dp", None, None),
            P("dp", None),
            P("dp", None),
            P(),
            P(),
        ),
        out_specs=(P("dp", "tm", "height", None, None), P(("tm", "height", "dp"), None)),
        check_vma=False,
    )
```

```python
import functools

import jax
import jax.numpy as jnp
from jax import lax
from jax.experimental import pallas as pl
from jax.experimental.pallas import tpu as pltpu
from jax.sharding import PartitionSpec as P

CORES = 2
PER = 2
MESH = pl.DeviceIdType.MESH
F32 = jnp.float32
BF16 = jnp.bfloat16


def nt(a, b):
    return lax.dot_general(a, b, (((1,), (1,)), ((), ())), preferred_element_type=F32)


def nn(a, b):
    return lax.dot_general(a, b, (((1,), (0,)), ((), ())), preferred_element_type=F32)


def tn(a, b):
    return lax.dot_general(a, b, (((0,), (0,)), ((), ())), preferred_element_type=F32)


def fused(
    X, Y, Z,
    clip_frames, acts, cot, weight, centre, spread, gain, bias,
    out, wout,
    act_in, act_send, act_all, cots, w_all, w_taps, lhs, grad, normed, slope,
    total, x_send, x_recv, row_sum, z_send, z_recv, s_send, s_recv, g_send, g_recv,
    act_sem, cot_sem, own_send, fwd_send, sis_send, halo_send, a_snd, a_rcv, w_snd, w_rcv,
    x_snd, x_rcv, z_snd, z_rcv, s_snd, s_rcv, g_snd, g_rcv, p_snd, p_rcv, z_ready,
):
    tm = lax.axis_index("tm")
    y = lax.axis_index("height")
    z = lax.axis_index("dp")
    x = tm // CORES
    c = tm % CORES
    span = CORES * PER
    cols, ch = cots.shape[2], cots.shape[3]
    chunk = act_all.shape[2]
    lead = 2
    halves = ch // 128

    def dev(xx, cc, yy, zz):
        return (xx * CORES + cc, yy, zz)

    def remote(src, dst, snd, rcv, target):
        return pltpu.make_async_remote_copy(
            src_ref=src, dst_ref=dst, send_sem=snd, recv_sem=rcv,
            device_id=target, device_id_type=MESH,
        )

    up, down = (y + 1) % Y, (y + Y - 1) % Y
    prev_x, next_x = (x + X - 1) % X, (x + 1) % X
    sister = dev(x, 1 - c, y, z)

    act_copy = pltpu.make_async_copy(acts, act_in, act_sem)
    act_copy.start()
    for k in range(PER):
        pltpu.make_async_copy(cot.at[k], cots.at[PER * c + k, y], cot_sem.at[PER * c + k, y]).start()

    barrier = pltpu.get_barrier_semaphore()
    partners = [
        dev(x, (c + dc) % CORES, (y + dy) % Y, z)
        for dc in range(CORES) for dy in range(Y) if dc or dy
    ]
    partners += [dev((x + dx) % X, c, y, z) for dx in range(1, X)]
    for target in partners:
        pl.semaphore_signal(barrier, inc=1, device_id=target, device_id_type=MESH)

    @pl.when(c == 0)
    def _():
        pl.semaphore_signal(barrier, inc=1, device_id=dev(prev_x, 1, y, z), device_id_type=MESH)

    @pl.when(c == 1)
    def _():
        pl.semaphore_signal(barrier, inc=1, device_id=dev(next_x, 0, y, z), device_id_type=MESH)

    for d in range(1, Z):
        @pl.when(z + d < Z)
        def _():
            pl.semaphore_signal(
                barrier, inc=1, device_id=dev(x, c, y, (z + d) % Z), device_id_type=MESH
            )

    row_id = lax.broadcasted_iota(jnp.int32, (ch, ch), 0)
    col_id = lax.broadcasted_iota(jnp.int32, (ch, ch), 1)
    half = ch // X
    per_core = half // CORES
    order = (
        ((row_id // Z) % X) * half + (row_id // (chunk * Y)) * per_core
        + ((row_id // chunk) % Y) * Z + row_id % Z
    )
    pick = jnp.where(order == col_id, 1.0, 0.0).astype(BF16)
    act_copy.wait()
    for k in range(PER):
        act_send[:, k] = nt(pick, act_in[k]).astype(BF16).reshape(CORES * Y, chunk, cols)

    pl.semaphore_wait(barrier, len(partners) + 1 + z)

    def cot_to(k, row, target, snd):
        src = cot.at[k] if row is None else cots.at[PER * c + k, row]
        at = y if row is None else row
        return remote(src, cots.at[PER * c + k, at], snd, cot_sem.at[PER * c + k, at], target)

    def halo_to(k, row, slot):
        src = cot.at[k] if row is None else cots.at[PER * c + k, row]
        at = y if row is None else row
        return remote(
            src, cots.at[span + k, at], halo_send.at[k, slot], cot_sem.at[span + k, at],
            dev(prev_x, k, y, z),
        )

    sends = []

    def go(copy):
        copy.start()
        sends.append(copy)

    around = [(dc, dy) for dc in range(CORES) for dy in range(Y) if dc or dy]
    for n, (dc, dy) in enumerate(around):
        cc, yy = (c + dc) % CORES, (y + dy) % Y
        go(remote(
            act_send.at[cc * Y + yy], act_all.at[pl.ds(lead + PER * c, PER), y], a_snd.at[n], a_rcv.at[n],
            dev(x, cc, yy, z),
        ))
    act_all[pl.ds(lead + PER * c, PER), y] = act_send[c * Y + y]

    for k in range(PER):
        ends = (up, down) if k == 0 else (down, up)
        for n, row in enumerate(ends):
            go(cot_to(k, None, dev(x, c, row, z), own_send.at[k, n]))
    for k in range(PER):
        go(cot_to(k, None, sister, sis_send.at[k, 0]))

        @pl.when(c == 0)
        def _():
            halo_to(k, None, 0).start()

    for d in range(1, Z):
        @pl.when(z >= d)
        def _():
            pl.semaphore_signal(
                z_ready, inc=1, device_id=dev(x, c, y, (z + Z - d) % Z), device_id_type=MESH
            )

    mine = (z % CORES) == c
    wsrc = weight.at[:, y]

    def weight_to(d):
        return remote(
            wsrc, w_all.at[:, z // CORES], w_snd.at[d - 1], w_rcv.at[z // CORES],
            dev(x, c, y, (z + d) % Z),
        )

    @pl.when(mine)
    def _():
        pltpu.make_async_copy(wsrc, w_all.at[:, z // CORES], w_rcv.at[z // CORES]).start()
        for d in range(1, Z):
            @pl.when(z + d >= Z)
            def _():
                weight_to(d).start()

    def clear(s, _):
        grad[s] = jnp.zeros(grad.shape[1:], F32)
        return 0

    def clear_edges(s, _):
        for edge in (0, Y + 1):
            lhs[s, edge] = jnp.zeros(lhs.shape[2:], BF16)
        return 0

    lax.fori_loop(0, span, clear, 0)
    lax.fori_loop(0, span + lead, clear_edges, 0)
    total[...] = jnp.zeros(total.shape, F32)

    def arrived(f, row):
        remote(
            cots.at[f, row], cots.at[f, row], own_send.at[0, 0], cot_sem.at[f, row], sister
        ).wait_recv()

    for n, (dc, dy) in enumerate(around):
        cs, ys = (c + dc) % CORES, (y + Y - dy) % Y
        remote(
            act_send.at[0], act_all.at[pl.ds(lead + PER * cs, PER), ys], a_snd.at[n], a_rcv.at[n], sister
        ).wait_recv()

    go(remote(
        act_all.at[pl.ds(span, lead)], act_all.at[pl.ds(0, lead)], p_snd, p_rcv, dev(next_x, c, y, z)
    ))

    i = lax.broadcasted_iota(jnp.int32, (chunk, 1), 0)
    channel = (i // Z) * half + c * per_core + y * Z + i % Z
    groups = centre.shape[1]
    group = (i // Z) * (groups // X) + c * (groups // X // CORES) + y

    def column(row, index):
        lane = lax.broadcasted_iota(jnp.int32, (chunk, row.shape[1]), 1)
        return jnp.sum(jnp.where(lane == index, row, 0.0), axis=1, keepdims=True)

    mean, scale = column(centre[...], group), column(spread[...], group)
    gains, biases = column(gain[...], channel), column(bias[...], channel)
    clip_len = clip_frames[0]

    def valid(f):
        t = x * span + f
        return jnp.where((t >= 0) & (t < clip_len), 1.0, 0.0).astype(F32)

    lane = lax.broadcasted_iota(jnp.int32, (chunk, cols), 1)

    def block_input(s, r):
        norm = (act_all[s + lead, r].astype(F32) - mean) * scale
        shifted = norm * gains + biases
        sig = jax.nn.sigmoid(shifted)
        a = shifted * sig * valid(s)
        at = s + lead
        lhs[at, r + 1, pl.ds(0, chunk)] = jnp.where(lane == 0, 0.0, pltpu.roll(a, 1, 1)).astype(BF16)
        lhs[at, r + 1, pl.ds(chunk, chunk)] = a.astype(BF16)
        lhs[at, r + 1, pl.ds(2 * chunk, chunk)] = jnp.where(
            lane == cols - 1, 0.0, pltpu.roll(a, cols - 1, 1)
        ).astype(BF16)
        return norm, shifted, sig

    def prepare(t, _):
        s, r = t // Y, t % Y
        norm, shifted, sig = block_input(s, r)
        normed[s, r] = norm
        slope[s, r] = sig * (1.0 + shifted * (1.0 - sig)) * valid(s) * gains
        return 0

    def prepare_before(t, _):
        block_input(t // Y - lead, t % Y)
        return 0

    lax.fori_loop(0, span * Y, prepare, 0)

    rows3 = lhs.shape[2]

    def taps_of(f):
        return max(0, lead - f), min(3, span + lead - f)

    def masked(f, r):
        return jnp.where(x * span + f < clip_len, cots[f, r], jnp.zeros((cols, ch), BF16))

    def weight_row(r):
        def body(f, _):
            @pl.when(c != f // PER)
            def _():
                arrived(f, r)

            left = lhs[pl.ds(f, 3), pl.ds(r, 3)].reshape(9 * rows3, cols)
            total[pl.ds(0, 27)] += nn(left, masked(f, r)).reshape(27, chunk, ch)
            return 0

        lax.fori_loop(0, span, body, 0)

    parts = [(t, min(8, 27 - t)) for t in range(0, 27, 8)]

    def sent_rows(taps):
        return -(-taps * Z // 16) * 16

    def reduce_x(j):
        tap, taps = parts[j]
        rows, whole = taps * Z, sent_rows(taps)
        for xx in range(X):
            x_send[j, xx, pl.ds(0, rows)] = (
                total[pl.ds(tap, taps), pl.ds(xx * Z, Z)].reshape(rows, ch).astype(BF16)
            )
            if whole > rows:
                x_send[j, xx, pl.ds(rows, whole - rows)] = jnp.zeros((whole - rows, ch), BF16)
        for d in range(1, X):
            xx = (x + d) % X
            go(remote(
                x_send.at[j, xx, pl.ds(0, whole)], x_recv.at[j, d - 1, pl.ds(0, whole)],
                x_snd.at[j, d - 1], x_rcv.at[j, d - 1], dev(xx, c, y, z),
            ))

    def reduce_z(j):
        tap, taps = parts[j]
        rows, whole = taps * Z, sent_rows(taps)
        for d in range(1, X):
            got = x_recv.at[j, d - 1, pl.ds(0, whole)]
            pltpu.make_async_copy(got, got, x_rcv.at[j, d - 1]).wait()
        part = total[pl.ds(tap, taps), pl.ds(x * Z, Z)].reshape(rows, ch)
        for d in range(1, X):
            part = part + x_recv[j, d - 1, pl.ds(0, rows)].astype(F32)
        for h in range(halves):
            row_sum[h, pl.ds(0, rows)] = part[:, h * 128 : (h + 1) * 128]
        for zz in range(Z):
            for h in range(halves):
                z_send[j, zz, :, pl.ds(h * 128, 128)] = row_sum[h, pl.ds(zz, 8, Z), :]
        for d in range(1, Z):
            zz = (z + d) % Z
            go(remote(
                z_send.at[j, zz], z_recv.at[j, d - 1], z_snd.at[j, d - 1], z_rcv.at[j, d - 1],
                dev(x, c, y, zz),
            ))


    across = (y + 2) % Y
    seen = [1, 1]

    def take(k, row, on):
        arrived(PER * c + k, row)
        if on is not None:
            go(cot_to(k, row, dev(x, c, on, z), fwd_send.at[k]))
        n = seen[k]
        seen[k] += 1
        go(cot_to(k, row, sister, sis_send.at[k, n]))

        @pl.when(c == 0)
        def _():
            halo_to(k, row, n).start()

    take(0, down, up)
    take(0, up, None)

    @pl.when(z < Z - 1)
    def _():
        pl.semaphore_wait(z_ready, Z - 1 - z)

    @pl.when(mine)
    def _():
        for d in range(1, Z):
            @pl.when(z + d < Z)
            def _():
                weight_to(d).start()

    pltpu.make_async_copy(act_all.at[pl.ds(0, lead)], act_all.at[pl.ds(0, lead)], p_rcv).wait()
    lax.fori_loop(0, lead * Y, prepare_before, 0)
    take(1, up, down)
    take(1, down, None)
    for k in range(PER):
        arrived(PER * c + k, y)

    def turn(n):
        return (y + n + (n // 2) * (1 - 2 * (n % 2))) % Y

    def early(n, _):
        weight_row(turn(n))
        return 0

    lax.fori_loop(0, Y - 1, early, 0)

    def halo_on(d):
        r = (y + d) % Y
        arrived(span + c, r)
        go(remote(
            cots.at[span + c, r], cots.at[span + c, r], fwd_send.at[PER + d], cot_sem.at[span + c, r],
            sister,
        ))

    halo_on(0)
    take(0, across, None)
    take(1, across, None)
    weight_row(across)
    row_sum[...] = jnp.zeros(row_sum.shape, F32)
    for j in range(len(parts)):
        reduce_x(j)
    halo_on(1)
    halo_on(3)

    for n in range(X):
        pltpu.make_async_copy(w_all.at[:, n], w_all.at[:, n], w_rcv.at[n]).wait()

    def by_tap(k, _):
        tap = w_all[pl.ds(3 * k, 3)].astype(F32).reshape(rows3, ch)
        w_taps[k // 3, k % 3] = tap.astype(BF16)
        return 0

    lax.fori_loop(0, 9, by_tap, 0)

    def input_term(f, r):
        k0, k1 = taps_of(f)
        s0, n = f - lead + k0, k1 - k0
        left = w_taps[pl.ds(k0, n)].reshape(n * 3 * rows3, ch)
        grad[pl.ds(s0, n), pl.ds(r, 3)] += nt(left, masked(f, r)).reshape(n, 3, rows3, cols)

    def input_row(r):
        for f in range(span):
            input_term(f, r)

    for n in range(Y - 1):
        input_row(turn(n))
        reduce_z(n)
    reduce_z(3)
    halo_on(2)
    input_row(across)
    for f in range(span, span + lead):
        def halo_input(r, _):
            @pl.when(c != f - span)
            def _():
                arrived(f, r)

            input_term(f, r)
            return 0

        lax.fori_loop(0, Y, halo_input, 0)

    def gather(t, carry):
        first, second = carry
        s, r = t // Y, t % Y
        g0 = grad[s, r + 1, pl.ds(0, chunk)]
        g1 = grad[s, r + 1, pl.ds(chunk, chunk)]
        g2 = grad[s, r + 1, pl.ds(2 * chunk, chunk)]
        whole = (
            jnp.where(lane == cols - 1, 0.0, pltpu.roll(g0, cols - 1, 1)) + g1
            + jnp.where(lane == 0, 0.0, pltpu.roll(g2, 1, 1))
        )
        upstream = whole * slope[s, r]
        slope[s, r] = upstream
        return first + upstream, second + upstream * normed[s, r]

    nothing = jnp.zeros((chunk, cols), F32)
    first, second = lax.fori_loop(0, span * Y, gather, (nothing, nothing))
    slim = lax.broadcasted_iota(jnp.int32, (chunk, 128), 1)
    first = jnp.sum(first, axis=1, keepdims=True)
    second = jnp.sum(second, axis=1, keepdims=True)
    s_send[...] = jnp.where(slim == 0, first, jnp.where(slim == 1, second, 0.0))
    for d in range(1, X):
        go(remote(
            s_send, s_recv.at[d - 1], s_snd.at[d - 1], s_rcv.at[d - 1], dev((x + d) % X, c, y, z)
        ))

    for d in range(1, X):
        pltpu.make_async_copy(s_recv.at[d - 1], s_recv.at[d - 1], s_rcv.at[d - 1]).wait()
    both = s_send[...]
    for d in range(1, X):
        both = both + s_recv[d - 1]
    both = both.reshape(X, Z, 128)
    both = jnp.broadcast_to(jnp.sum(both, axis=1, keepdims=True), (X, Z, 128)).reshape(chunk, 128)
    population = clip_len.astype(F32) * (Y * cols * Z)
    first = jnp.sum(jnp.where(slim == 0, both, 0.0), axis=1, keepdims=True) / population
    second = jnp.sum(jnp.where(slim == 1, both, 0.0), axis=1, keepdims=True) / population

    def finish(t, _):
        s, r = t // Y, t % Y
        value = scale * (slope[s, r] - first - normed[s, r] * second) * valid(s)
        g_send[s, r] = value.astype(BF16)
        return 0

    lax.fori_loop(0, span * Y, finish, 0)
    for n, (dc, dy) in enumerate(around):
        cc, yy = (c + dc) % CORES, (y + dy) % Y
        go(remote(
            g_send.at[pl.ds(PER * cc, PER), yy], g_recv.at[c * Y + y], g_snd.at[n], g_rcv.at[n],
            dev(x, cc, yy, z),
        ))
    g_recv[c * Y + y] = g_send[pl.ds(PER * c, PER), y]

    final = z_send[:, z]
    for j in range(len(parts)):
        for d in range(1, Z):
            pltpu.make_async_copy(z_recv.at[j, d - 1], z_recv.at[j, d - 1], z_rcv.at[j, d - 1]).wait()
    for d in range(1, Z):
        final = final + z_recv[:, d - 1]
    final = final.reshape(len(parts) * 8, ch)[:27]
    cells = X * Y * Z * CORES * PER * cols
    wout[...] = (final * (1.0 / cells)).astype(BF16)

    for n, (dc, dy) in enumerate(around):
        cs, ys = (c + dc) % CORES, (y + Y - dy) % Y
        remote(
            g_send.at[pl.ds(0, PER), 0], g_recv.at[cs * Y + ys], g_snd.at[n], g_rcv.at[n], sister
        ).wait_recv()
    for k in range(PER):
        out[k] = tn(g_recv[:, k].reshape(ch, cols), pick).astype(BF16)

    for copy in sends:
        copy.wait_send()

    @pl.when(c == 0)
    def _():
        for k in range(PER):
            for n in range(Y):
                halo_to(k, y, n).wait_send()

    @pl.when(mine)
    def _():
        for d in range(1, Z):
            weight_to(d).wait_send()


def per_device(X, Y, Z, acts, cot, clip_frames, weight, centre, spread, gain, bias):
    _, per, _, cols, ch = acts.shape
    span, lead = CORES * per, 2
    chunk = ch // (CORES * Y)
    taps = weight.shape[1]
    dma = pltpu.SemaphoreType.DMA
    hbm = pl.BlockSpec(memory_space=pl.ANY)
    vmem = pl.BlockSpec(memory_space=pltpu.VMEM)
    grad_input, weight_grad = pl.pallas_call(
        functools.partial(fused, X, Y, Z),
        out_shape=(
            jax.ShapeDtypeStruct((per, cols, ch), BF16),
            jax.ShapeDtypeStruct((taps, ch), BF16),
        ),
        in_specs=[pl.BlockSpec(memory_space=pltpu.SMEM), hbm, hbm, hbm, vmem, vmem, vmem, vmem],
        out_specs=(vmem, vmem),
        scratch_shapes=[
            pltpu.VMEM((per, cols, ch), BF16),
            pltpu.VMEM((CORES * Y, per, chunk, cols), BF16),
            pltpu.VMEM((span + lead, Y, chunk, cols), BF16),
            pltpu.VMEM((span + lead, Y, cols, ch), BF16),
            pltpu.VMEM((taps, X, Z, ch), BF16),
            pltpu.VMEM((3, 3, 3 * chunk, ch), BF16),
            pltpu.VMEM((span + lead, Y + 2, 3 * chunk, cols), BF16),
            pltpu.VMEM((span, Y + 2, 3 * chunk, cols), F32),
            pltpu.VMEM((span, Y, chunk, cols), F32),
            pltpu.VMEM((span, Y, chunk, cols), F32),
            pltpu.VMEM((taps, chunk, ch), F32),
            pltpu.VMEM((4, X, 8 * Z, ch), BF16),
            pltpu.VMEM((4, X - 1, 8 * Z, ch), BF16),
            pltpu.VMEM((ch // 128, 8 * Z, 128), F32),
            pltpu.VMEM((4, Z, 8, ch), F32),
            pltpu.VMEM((4, Z - 1, 8, ch), F32),
            pltpu.VMEM((chunk, 128), F32),
            pltpu.VMEM((X - 1, chunk, 128), F32),
            pltpu.VMEM((span, Y, chunk, cols), BF16),
            pltpu.VMEM((CORES * Y, per, chunk, cols), BF16),
            dma,
            dma((span + lead, Y)),
            dma((per, 2)),
            dma((per + Y,)),
            dma((per, Y)),
            dma((per, Y)),
            dma((CORES * Y - 1,)),
            dma((CORES * Y - 1,)),
            dma((Z - 1,)),
            dma((X,)),
            dma((4, X - 1)),
            dma((4, X - 1)),
            dma((4, Z - 1)),
            dma((4, Z - 1)),
            dma((X - 1,)),
            dma((X - 1,)),
            dma((CORES * Y - 1,)),
            dma((CORES * Y - 1,)),
            dma,
            dma,
            pltpu.SemaphoreType.REGULAR,
        ],
        compiler_params=pltpu.CompilerParams(
            collective_id=0, has_side_effects=True, vmem_limit_bytes=60 * 1024 * 1024
        ),
    )(
        clip_frames,
        acts.reshape(per, cols, ch),
        cot.reshape(per, cols, ch),
        weight.transpose(1, 0, 2).reshape(taps, Y, Z, ch),
        centre,
        spread,
        gain.reshape(1, ch),
        bias.reshape(1, ch),
    )
    return grad_input.reshape(1, per, 1, cols, ch), weight_grad


def solution(mesh):
    X, Y, Z = mesh.shape["tm"] // CORES, mesh.shape["height"], mesh.shape["dp"]
    return jax.shard_map(
        functools.partial(per_device, X, Y, Z),
        mesh=mesh,
        in_specs=(
            P("dp", "tm", "height", None, None),
            P("dp", "tm", "height", None, None),
            P("dp"),
            P("dp", None, None),
            P("dp", None),
            P("dp", None),
            P(),
            P(),
        ),
        out_specs=(P("dp", "tm", "height", None, None), P(("tm", "height", "dp"), None)),
        check_vma=False,
    )
```

```python
import functools

import jax
import jax.numpy as jnp
from jax import lax
from jax.experimental import pallas as pl
from jax.experimental.pallas import tpu as pltpu
from jax.sharding import PartitionSpec as P

CORES = 2
PER = 2
MESH = pl.DeviceIdType.MESH
F32 = jnp.float32
BF16 = jnp.bfloat16


def nt(a, b):
    return lax.dot_general(a, b, (((1,), (1,)), ((), ())), preferred_element_type=F32)


def nn(a, b):
    return lax.dot_general(a, b, (((1,), (0,)), ((), ())), preferred_element_type=F32)


def tn(a, b):
    return lax.dot_general(a, b, (((0,), (0,)), ((), ())), preferred_element_type=F32)


def fused(
    X, Y, Z,
    clip_frames, acts, cot, weight, centre, spread, gain, bias,
    out, wout,
    act_in, act_send, act_mid, act_all, cots, w_all, w_taps, lhs, grad, normed, slope,
    total, x_send, x_recv, row_sum, z_send, z_recv, s_send, s_recv, g_send, g_mid, g_recv,
    act_sem, cot_sem, own_send, fwd_send, sis_send, halo_send, a_snd, a_rcv, w_snd, w_rcv,
    x_snd, x_rcv, z_snd, z_rcv, s_snd, s_rcv, g_snd, g_rcv, p_snd, p_rcv, z_ready,
):
    tm = lax.axis_index("tm")
    y = lax.axis_index("height")
    z = lax.axis_index("dp")
    x = tm // CORES
    c = tm % CORES
    span = CORES * PER
    cols, ch = cots.shape[2], cots.shape[3]
    chunk = act_all.shape[2]
    lead = 2
    halves = ch // 128

    def dev(xx, cc, yy, zz):
        return (xx * CORES + cc, yy, zz)

    def remote(src, dst, snd, rcv, target):
        return pltpu.make_async_remote_copy(
            src_ref=src, dst_ref=dst, send_sem=snd, recv_sem=rcv,
            device_id=target, device_id_type=MESH,
        )

    up, down = (y + 1) % Y, (y + Y - 1) % Y
    prev_x, next_x = (x + X - 1) % X, (x + 1) % X
    sister = dev(x, 1 - c, y, z)

    act_copy = pltpu.make_async_copy(acts, act_in, act_sem)
    act_copy.start()
    for k in range(PER):
        pltpu.make_async_copy(cot.at[k], cots.at[PER * c + k, y], cot_sem.at[PER * c + k, y]).start()

    barrier = pltpu.get_barrier_semaphore()
    partners = [sister] + [dev(x, c, (y + dy) % Y, z) for dy in range(1, Y)]
    partners += [dev((x + dx) % X, c, y, z) for dx in range(1, X)]
    for target in partners:
        pl.semaphore_signal(barrier, inc=1, device_id=target, device_id_type=MESH)

    for d in range(1, Z):
        @pl.when(z + d < Z)
        def _():
            pl.semaphore_signal(
                barrier, inc=1, device_id=dev(x, c, y, (z + d) % Z), device_id_type=MESH
            )

    row_id = lax.broadcasted_iota(jnp.int32, (ch, ch), 0)
    col_id = lax.broadcasted_iota(jnp.int32, (ch, ch), 1)
    half = ch // X
    per_core = half // CORES
    order = (
        ((row_id // Z) % X) * half + (row_id // (chunk * Y)) * per_core
        + ((row_id // chunk) % Y) * Z + row_id % Z
    )
    pick = jnp.where(order == col_id, 1.0, 0.0).astype(BF16)
    act_copy.wait()
    for k in range(PER):
        act_send[:, k] = nt(pick, act_in[k]).astype(BF16).reshape(CORES * Y, chunk, cols)

    pl.semaphore_wait(barrier, len(partners) + z)

    def cot_to(k, row, target, snd):
        src = cot.at[k] if row is None else cots.at[PER * c + k, row]
        at = y if row is None else row
        return remote(src, cots.at[PER * c + k, at], snd, cot_sem.at[PER * c + k, at], target)

    def halo_to(row, slot):
        return remote(
            cots.at[c, row], cots.at[span + c, row], halo_send.at[slot], cot_sem.at[span + c, row],
            dev(prev_x, c, y, z),
        )

    sends = []

    def go(copy):
        copy.start()
        sends.append(copy)

    def arrived(f, row):
        remote(
            cots.at[f, row], cots.at[f, row], own_send.at[0, 0], cot_sem.at[f, row], sister
        ).wait_recv()

    def blocks_to(n, src, core, dy):
        return remote(
            src, act_all.at[pl.ds(lead + PER * core, PER), y], a_snd.at[n], a_rcv.at[n],
            dev(x, c, (y + dy) % Y, z),
        )

    go(remote(
        act_send.at[pl.ds((1 - c) * Y, Y)], act_mid, a_snd.at[0], a_rcv.at[0], sister
    ))
    for k in range(PER):
        go(cot_to(k, None, sister, sis_send.at[k, 0]))
    for dy in range(1, Y):
        go(blocks_to(dy, act_send.at[c * Y + (y + dy) % Y], c, dy))
    for k in range(PER):
        ends = (up, down) if k == 0 else (down, up)
        for n, row in enumerate(ends):
            go(cot_to(k, None, dev(x, c, row, z), own_send.at[k, n]))
    act_all[pl.ds(lead + PER * c, PER), y] = act_send[c * Y + y]
    mid = remote(act_mid, act_mid, a_snd.at[0], a_rcv.at[0], sister)
    mid.wait_recv()
    for dy in range(1, Y):
        go(blocks_to(Y - 1 + dy, act_mid.at[(y + dy) % Y], 1 - c, dy))
    act_all[pl.ds(lead + PER * (1 - c), PER), y] = act_mid[y]

    for d in range(1, Z):
        @pl.when(z >= d)
        def _():
            pl.semaphore_signal(
                z_ready, inc=1, device_id=dev(x, c, y, (z + Z - d) % Z), device_id_type=MESH
            )

    mine = (z % CORES) == c
    wsrc = weight.at[:, y]

    def weight_to(d):
        return remote(
            wsrc, w_all.at[:, z // CORES], w_snd.at[d - 1], w_rcv.at[z // CORES],
            dev(x, c, y, (z + d) % Z),
        )

    @pl.when(mine)
    def _():
        pltpu.make_async_copy(wsrc, w_all.at[:, z // CORES], w_rcv.at[z // CORES]).start()
        for d in range(1, Z):
            @pl.when(z + d >= Z)
            def _():
                weight_to(d).start()

    def clear(s, _):
        grad[s] = jnp.zeros(grad.shape[1:], F32)
        return 0

    def clear_edges(s, _):
        for edge in (0, Y + 1):
            lhs[s, edge] = jnp.zeros(lhs.shape[2:], BF16)
        return 0

    lax.fori_loop(0, span, clear, 0)
    lax.fori_loop(0, span + lead, clear_edges, 0)
    total[...] = jnp.zeros(total.shape, F32)

    for k in range(PER):
        arrived(PER * c + k, y)

    def halo_late(row, slot):
        @pl.when(c == 1)
        def _():
            arrived(1, row)
            halo_to(row, slot).start()

    @pl.when(c == 0)
    def _():
        halo_to(y, 0).start()

    halo_late(y, 0)
    for dy in range(1, Y):
        for n, core in ((dy, c), (Y - 1 + dy, 1 - c)):
            blocks = act_all.at[pl.ds(lead + PER * core, PER), (y + Y - dy) % Y]
            remote(blocks, blocks, a_snd.at[n], a_rcv.at[n], sister).wait_recv()
    go(remote(
        act_all.at[pl.ds(span, lead)], act_all.at[pl.ds(0, lead)], p_snd, p_rcv, dev(next_x, c, y, z)
    ))

    i = lax.broadcasted_iota(jnp.int32, (chunk, 1), 0)
    channel = (i // Z) * half + c * per_core + y * Z + i % Z
    groups = centre.shape[1]
    group = (i // Z) * (groups // X) + c * (groups // X // CORES) + y

    def column(row, index):
        lane = lax.broadcasted_iota(jnp.int32, (chunk, row.shape[1]), 1)
        return jnp.sum(jnp.where(lane == index, row, 0.0), axis=1, keepdims=True)

    mean, scale = column(centre[...], group), column(spread[...], group)
    gains, biases = column(gain[...], channel), column(bias[...], channel)
    clip_len = clip_frames[0]

    def valid(f):
        t = x * span + f
        return jnp.where((t >= 0) & (t < clip_len), 1.0, 0.0).astype(F32)

    lane = lax.broadcasted_iota(jnp.int32, (chunk, cols), 1)

    def block_input(s, r):
        norm = (act_all[s + lead, r].astype(F32) - mean) * scale
        shifted = norm * gains + biases
        sig = jax.nn.sigmoid(shifted)
        a = shifted * sig * valid(s)
        at = s + lead
        lhs[at, r + 1, pl.ds(0, chunk)] = jnp.where(lane == 0, 0.0, pltpu.roll(a, 1, 1)).astype(BF16)
        lhs[at, r + 1, pl.ds(chunk, chunk)] = a.astype(BF16)
        lhs[at, r + 1, pl.ds(2 * chunk, chunk)] = jnp.where(
            lane == cols - 1, 0.0, pltpu.roll(a, cols - 1, 1)
        ).astype(BF16)
        return norm, shifted, sig

    def prepare(t, _):
        s, r = t // Y, t % Y
        norm, shifted, sig = block_input(s, r)
        normed[s, r] = norm
        slope[s, r] = sig * (1.0 + shifted * (1.0 - sig)) * valid(s) * gains
        return 0

    def prepare_before(t, _):
        block_input(t // Y - lead, t % Y)
        return 0

    lax.fori_loop(0, span * Y, prepare, 0)

    rows3 = lhs.shape[2]

    def taps_of(f):
        return max(0, lead - f), min(3, span + lead - f)

    def masked(f, r):
        return jnp.where(x * span + f < clip_len, cots[f, r], jnp.zeros((cols, ch), BF16))

    def weight_row(r):
        def body(f, _):
            @pl.when((c != f // PER) & ((c == 0) | (f != 1)))
            def _():
                arrived(f, r)

            left = lhs[pl.ds(f, 3), pl.ds(r, 3)].reshape(9 * rows3, cols)
            total[pl.ds(0, 27)] += nn(left, masked(f, r)).reshape(27, chunk, ch)
            return 0

        lax.fori_loop(0, span, body, 0)

    parts = [(t, min(8, 27 - t)) for t in range(0, 27, 8)]

    def sent_rows(taps):
        return -(-taps * Z // 16) * 16

    def reduce_x(j):
        tap, taps = parts[j]
        rows, whole = taps * Z, sent_rows(taps)
        for xx in range(X):
            x_send[j, xx, pl.ds(0, rows)] = (
                total[pl.ds(tap, taps), pl.ds(xx * Z, Z)].reshape(rows, ch).astype(BF16)
            )
            if whole > rows:
                x_send[j, xx, pl.ds(rows, whole - rows)] = jnp.zeros((whole - rows, ch), BF16)
        for d in range(1, X):
            xx = (x + d) % X
            go(remote(
                x_send.at[j, xx, pl.ds(0, whole)], x_recv.at[j, d - 1, pl.ds(0, whole)],
                x_snd.at[j, d - 1], x_rcv.at[j, d - 1], dev(xx, c, y, z),
            ))

    def reduce_z(j):
        tap, taps = parts[j]
        rows, whole = taps * Z, sent_rows(taps)
        for d in range(1, X):
            got = x_recv.at[j, d - 1, pl.ds(0, whole)]
            pltpu.make_async_copy(got, got, x_rcv.at[j, d - 1]).wait()
        part = total[pl.ds(tap, taps), pl.ds(x * Z, Z)].reshape(rows, ch)
        for d in range(1, X):
            part = part + x_recv[j, d - 1, pl.ds(0, rows)].astype(F32)
        for h in range(halves):
            row_sum[h, pl.ds(0, rows)] = part[:, h * 128 : (h + 1) * 128]
        for zz in range(Z):
            for h in range(halves):
                z_send[j, zz, :, pl.ds(h * 128, 128)] = row_sum[h, pl.ds(zz, 8, Z), :]
        for d in range(1, Z):
            zz = (z + d) % Z
            go(remote(
                z_send.at[j, zz], z_recv.at[j, d - 1], z_snd.at[j, d - 1], z_rcv.at[j, d - 1],
                dev(x, c, y, zz),
            ))


    across = (y + 2) % Y
    seen = [1, 1]

    def take(k, row, on):
        arrived(PER * c + k, row)
        if on is not None:
            go(cot_to(k, row, dev(x, c, on, z), fwd_send.at[k]))
        n = seen[k]
        seen[k] += 1
        go(cot_to(k, row, sister, sis_send.at[k, n]))

        if k == 0:
            @pl.when(c == 0)
            def _():
                halo_to(row, n).start()

    take(0, down, up)
    take(0, up, None)

    @pl.when(z < Z - 1)
    def _():
        pl.semaphore_wait(z_ready, Z - 1 - z)

    @pl.when(mine)
    def _():
        for d in range(1, Z):
            @pl.when(z + d < Z)
            def _():
                weight_to(d).start()

    pltpu.make_async_copy(act_all.at[pl.ds(0, lead)], act_all.at[pl.ds(0, lead)], p_rcv).wait()
    lax.fori_loop(0, lead * Y, prepare_before, 0)
    take(1, up, down)
    take(1, down, None)
    halo_late(down, 1)
    halo_late(up, 2)

    def turn(n):
        return (y + n + (n // 2) * (1 - 2 * (n % 2))) % Y

    def early(n, _):
        weight_row(turn(n))
        return 0

    lax.fori_loop(0, Y - 1, early, 0)

    def halo_on(d):
        r = (y + d) % Y
        arrived(span + c, r)
        go(remote(
            cots.at[span + c, r], cots.at[span + c, r], fwd_send.at[PER + d], cot_sem.at[span + c, r],
            sister,
        ))

    halo_on(0)
    take(0, across, None)
    take(1, across, None)
    halo_late(across, 3)
    weight_row(across)
    row_sum[...] = jnp.zeros(row_sum.shape, F32)
    for j in range(len(parts)):
        reduce_x(j)

    for n in range(X):
        pltpu.make_async_copy(w_all.at[:, n], w_all.at[:, n], w_rcv.at[n]).wait()

    def by_tap(k, _):
        tap = w_all[pl.ds(3 * k, 3)].astype(F32).reshape(rows3, ch)
        w_taps[k // 3, k % 3] = tap.astype(BF16)
        return 0

    lax.fori_loop(0, 9, by_tap, 0)

    def input_term(f, r):
        k0, k1 = taps_of(f)
        s0, n = f - lead + k0, k1 - k0
        left = w_taps[pl.ds(k0, n)].reshape(n * 3 * rows3, ch)
        grad[pl.ds(s0, n), pl.ds(r, 3)] += nt(left, masked(f, r)).reshape(n, 3, rows3, cols)

    def input_row(r):
        for f in range(span):
            input_term(f, r)

    def input_rows(n, _):
        input_row(turn(n))
        return 0

    lax.fori_loop(0, 2, input_rows, 0)
    halo_on(1)
    halo_on(3)
    lax.fori_loop(2, Y, input_rows, 0)

    def gather(t, carry):
        first, second = carry
        s, r = t // Y, t % Y
        g0 = grad[s, r + 1, pl.ds(0, chunk)]
        g1 = grad[s, r + 1, pl.ds(chunk, chunk)]
        g2 = grad[s, r + 1, pl.ds(2 * chunk, chunk)]
        whole = (
            jnp.where(lane == cols - 1, 0.0, pltpu.roll(g0, cols - 1, 1)) + g1
            + jnp.where(lane == 0, 0.0, pltpu.roll(g2, 1, 1))
        )
        upstream = whole * slope[s, r]
        slope[s, r] = upstream
        return first + upstream, second + upstream * normed[s, r]

    nothing = jnp.zeros((chunk, cols), F32)
    early_sums = lax.fori_loop(0, (span - lead) * Y, gather, (nothing, nothing))
    halo_on(2)
    for f in range(span, span + lead):
        def halo_input(r, _):
            @pl.when(c != f - span)
            def _():
                arrived(f, r)

            input_term(f, r)
            return 0

        lax.fori_loop(0, Y, halo_input, 0)
    first, second = lax.fori_loop((span - lead) * Y, span * Y, gather, early_sums)
    slim = lax.broadcasted_iota(jnp.int32, (chunk, 128), 1)
    first = jnp.sum(first, axis=1, keepdims=True)
    second = jnp.sum(second, axis=1, keepdims=True)
    s_send[...] = jnp.where(slim == 0, first, jnp.where(slim == 1, second, 0.0))
    for d in range(1, X):
        go(remote(
            s_send, s_recv.at[d - 1], s_snd.at[d - 1], s_rcv.at[d - 1], dev((x + d) % X, c, y, z)
        ))

    for j in range(len(parts)):
        reduce_z(j)

    for d in range(1, X):
        pltpu.make_async_copy(s_recv.at[d - 1], s_recv.at[d - 1], s_rcv.at[d - 1]).wait()
    both = s_send[...]
    for d in range(1, X):
        both = both + s_recv[d - 1]
    both = both.reshape(X, Z, 128)
    both = jnp.broadcast_to(jnp.sum(both, axis=1, keepdims=True), (X, Z, 128)).reshape(chunk, 128)
    population = clip_len.astype(F32) * (Y * cols * Z)
    first = jnp.sum(jnp.where(slim == 0, both, 0.0), axis=1, keepdims=True) / population
    second = jnp.sum(jnp.where(slim == 1, both, 0.0), axis=1, keepdims=True) / population

    def finish(core):
        def body(t, _):
            s, r = PER * core + t // Y, t % Y
            value = scale * (slope[s, r] - first - normed[s, r] * second) * valid(s)
            g_send[s, r] = value.astype(BF16)
            return 0

        lax.fori_loop(0, PER * Y, body, 0)

    finish(1 - c)
    go(remote(g_send.at[pl.ds(PER * (1 - c), PER)], g_mid, g_snd.at[0], g_rcv.at[0], sister))
    finish(c)

    def rows_to(n, src, core, dy):
        return remote(
            src, g_recv.at[core * Y + y], g_snd.at[n], g_rcv.at[n], dev(x, c, (y + dy) % Y, z)
        )

    for dy in range(1, Y):
        go(rows_to(dy, g_send.at[pl.ds(PER * c, PER), (y + dy) % Y], c, dy))
    g_recv[c * Y + y] = g_send[pl.ds(PER * c, PER), y]
    remote(g_mid, g_mid, g_snd.at[0], g_rcv.at[0], sister).wait_recv()
    for dy in range(1, Y):
        go(rows_to(Y - 1 + dy, g_mid.at[:, (y + dy) % Y], 1 - c, dy))
    g_recv[(1 - c) * Y + y] = g_mid[:, y]

    final = z_send[:, z]
    for j in range(len(parts)):
        for d in range(1, Z):
            pltpu.make_async_copy(z_recv.at[j, d - 1], z_recv.at[j, d - 1], z_rcv.at[j, d - 1]).wait()
    for d in range(1, Z):
        final = final + z_recv[:, d - 1]
    final = final.reshape(len(parts) * 8, ch)[:27]
    cells = X * Y * Z * CORES * PER * cols
    wout[...] = (final * (1.0 / cells)).astype(BF16)

    for dy in range(1, Y):
        for n, core in ((dy, c), (Y - 1 + dy, 1 - c)):
            rows = g_recv.at[core * Y + (y + Y - dy) % Y]
            remote(rows, rows, g_snd.at[n], g_rcv.at[n], sister).wait_recv()
    for k in range(PER):
        out[k] = tn(g_recv[:, k].reshape(ch, cols), pick).astype(BF16)

    for copy in sends:
        copy.wait_send()

    for n in range(Y):
        halo_to(y, n).wait_send()

    @pl.when(mine)
    def _():
        for d in range(1, Z):
            weight_to(d).wait_send()


def per_device(X, Y, Z, acts, cot, clip_frames, weight, centre, spread, gain, bias):
    _, per, _, cols, ch = acts.shape
    span, lead = CORES * per, 2
    chunk = ch // (CORES * Y)
    taps = weight.shape[1]
    dma = pltpu.SemaphoreType.DMA
    hbm = pl.BlockSpec(memory_space=pl.ANY)
    vmem = pl.BlockSpec(memory_space=pltpu.VMEM)
    grad_input, weight_grad = pl.pallas_call(
        functools.partial(fused, X, Y, Z),
        out_shape=(
            jax.ShapeDtypeStruct((per, cols, ch), BF16),
            jax.ShapeDtypeStruct((taps, ch), BF16),
        ),
        in_specs=[pl.BlockSpec(memory_space=pltpu.SMEM), hbm, hbm, hbm, vmem, vmem, vmem, vmem],
        out_specs=(vmem, vmem),
        scratch_shapes=[
            pltpu.VMEM((per, cols, ch), BF16),
            pltpu.VMEM((CORES * Y, per, chunk, cols), BF16),
            pltpu.VMEM((Y, per, chunk, cols), BF16),
            pltpu.VMEM((span + lead, Y, chunk, cols), BF16),
            pltpu.VMEM((span + lead, Y, cols, ch), BF16),
            pltpu.VMEM((taps, X, Z, ch), BF16),
            pltpu.VMEM((3, 3, 3 * chunk, ch), BF16),
            pltpu.VMEM((span + lead, Y + 2, 3 * chunk, cols), BF16),
            pltpu.VMEM((span, Y + 2, 3 * chunk, cols), F32),
            pltpu.VMEM((span, Y, chunk, cols), F32),
            pltpu.VMEM((span, Y, chunk, cols), F32),
            pltpu.VMEM((taps, chunk, ch), F32),
            pltpu.VMEM((4, X, 8 * Z, ch), BF16),
            pltpu.VMEM((4, X - 1, 8 * Z, ch), BF16),
            pltpu.VMEM((ch // 128, 8 * Z, 128), F32),
            pltpu.VMEM((4, Z, 8, ch), F32),
            pltpu.VMEM((4, Z - 1, 8, ch), F32),
            pltpu.VMEM((chunk, 128), F32),
            pltpu.VMEM((X - 1, chunk, 128), F32),
            pltpu.VMEM((span, Y, chunk, cols), BF16),
            pltpu.VMEM((per, Y, chunk, cols), BF16),
            pltpu.VMEM((CORES * Y, per, chunk, cols), BF16),
            dma,
            dma((span + lead, Y)),
            dma((per, 2)),
            dma((per + Y,)),
            dma((per, Y)),
            dma((Y,)),
            dma((CORES * Y - 1,)),
            dma((CORES * Y - 1,)),
            dma((Z - 1,)),
            dma((X,)),
            dma((4, X - 1)),
            dma((4, X - 1)),
            dma((4, Z - 1)),
            dma((4, Z - 1)),
            dma((X - 1,)),
            dma((X - 1,)),
            dma((CORES * Y - 1,)),
            dma((CORES * Y - 1,)),
            dma,
            dma,
            pltpu.SemaphoreType.REGULAR,
        ],
        compiler_params=pltpu.CompilerParams(
            collective_id=0, has_side_effects=True, vmem_limit_bytes=60 * 1024 * 1024
        ),
    )(
        clip_frames,
        acts.reshape(per, cols, ch),
        cot.reshape(per, cols, ch),
        weight.transpose(1, 0, 2).reshape(taps, Y, Z, ch),
        centre,
        spread,
        gain.reshape(1, ch),
        bias.reshape(1, ch),
    )
    return grad_input.reshape(1, per, 1, cols, ch), weight_grad


def solution(mesh):
    X, Y, Z = mesh.shape["tm"] // CORES, mesh.shape["height"], mesh.shape["dp"]
    return jax.shard_map(
        functools.partial(per_device, X, Y, Z),
        mesh=mesh,
        in_specs=(
            P("dp", "tm", "height", None, None),
            P("dp", "tm", "height", None, None),
            P("dp"),
            P("dp", None, None),
            P("dp", None),
            P("dp", None),
            P(),
            P(),
        ),
        out_specs=(P("dp", "tm", "height", None, None), P(("tm", "height", "dp"), None)),
        check_vma=False,
    )
```

```python
import functools

import jax
import jax.numpy as jnp
from jax import lax
from jax.experimental import pallas as pl
from jax.experimental.pallas import tpu as pltpu
from jax.sharding import PartitionSpec as P

CORES = 2
PER = 2
MESH = pl.DeviceIdType.MESH
F32 = jnp.float32
BF16 = jnp.bfloat16


def nt(a, b):
    return lax.dot_general(a, b, (((1,), (1,)), ((), ())), preferred_element_type=F32)


def nn(a, b):
    return lax.dot_general(a, b, (((1,), (0,)), ((), ())), preferred_element_type=F32)


def tn(a, b):
    return lax.dot_general(a, b, (((0,), (0,)), ((), ())), preferred_element_type=F32)


def fused(
    X, Y, Z,
    clip_frames, acts, cot, weight, centre, spread, gain, bias,
    out, wout,
    act_in, act_send, act_mid, act_all, cots, w_all, w_taps, lhs, grad, normed, slope,
    total, x_send, x_recv, row_sum, z_send, z_recv, s_send, s_recv, g_send, g_mid, g_recv,
    act_sem, cot_sem, own_send, fwd_send, sis_send, halo_send, a_snd, a_rcv, w_snd, w_rcv,
    x_snd, x_rcv, z_snd, z_rcv, s_snd, s_rcv, g_snd, g_rcv, p_snd, p_rcv, z_ready,
):
    tm = lax.axis_index("tm")
    y = lax.axis_index("height")
    z = lax.axis_index("dp")
    x = tm // CORES
    c = tm % CORES
    span = CORES * PER
    cols, ch = cots.shape[2], cots.shape[3]
    chunk = act_all.shape[2]
    lead = 2
    halves = ch // 128

    def dev(xx, cc, yy, zz):
        return (xx * CORES + cc, yy, zz)

    def remote(src, dst, snd, rcv, target):
        return pltpu.make_async_remote_copy(
            src_ref=src, dst_ref=dst, send_sem=snd, recv_sem=rcv,
            device_id=target, device_id_type=MESH,
        )

    up, down = (y + 1) % Y, (y + Y - 1) % Y
    prev_x, next_x = (x + X - 1) % X, (x + 1) % X
    sister = dev(x, 1 - c, y, z)

    act_copy = pltpu.make_async_copy(acts, act_in, act_sem)
    act_copy.start()
    for k in range(PER):
        pltpu.make_async_copy(cot.at[k], cots.at[PER * c + k, y], cot_sem.at[PER * c + k, y]).start()

    barrier = pltpu.get_barrier_semaphore()
    partners = [sister] + [dev(x, c, (y + dy) % Y, z) for dy in range(1, Y)]
    partners += [dev((x + dx) % X, c, y, z) for dx in range(1, X)]
    for target in partners:
        pl.semaphore_signal(barrier, inc=1, device_id=target, device_id_type=MESH)

    for d in range(1, Z):
        @pl.when(z + d < Z)
        def _():
            pl.semaphore_signal(
                barrier, inc=1, device_id=dev(x, c, y, (z + d) % Z), device_id_type=MESH
            )

    row_id = lax.broadcasted_iota(jnp.int32, (ch, ch), 0)
    col_id = lax.broadcasted_iota(jnp.int32, (ch, ch), 1)
    half = ch // X
    per_core = half // CORES
    order = (
        ((row_id // Z) % X) * half + (row_id // (chunk * Y)) * per_core
        + ((row_id // chunk) % Y) * Z + row_id % Z
    )
    pick = jnp.where(order == col_id, 1.0, 0.0).astype(BF16)
    act_copy.wait()
    for k in range(PER):
        act_send[:, k] = nt(pick, act_in[k]).astype(BF16).reshape(CORES * Y, chunk, cols)

    pl.semaphore_wait(barrier, len(partners) + z)

    def cot_to(k, row, target, snd):
        src = cot.at[k] if row is None else cots.at[PER * c + k, row]
        at = y if row is None else row
        return remote(src, cots.at[PER * c + k, at], snd, cot_sem.at[PER * c + k, at], target)

    def halo_to(row, slot):
        return remote(
            cots.at[c, row], cots.at[span + c, row], halo_send.at[slot], cot_sem.at[span + c, row],
            dev(prev_x, c, y, z),
        )

    sends = []

    def go(copy):
        copy.start()
        sends.append(copy)

    def arrived(f, row):
        remote(
            cots.at[f, row], cots.at[f, row], own_send.at[0, 0], cot_sem.at[f, row], sister
        ).wait_recv()

    def blocks_to(n, src, core, dy):
        return remote(
            src, act_all.at[pl.ds(lead + PER * core, PER), y], a_snd.at[n], a_rcv.at[n],
            dev(x, c, (y + dy) % Y, z),
        )

    for d in range(1, Z):
        @pl.when(z >= d)
        def _():
            pl.semaphore_signal(
                z_ready, inc=1, device_id=dev(x, c, y, (z + Z - d) % Z), device_id_type=MESH
            )

    mine = (z % CORES) == c
    wsrc = weight.at[:, y]

    def weight_to(d):
        return remote(
            wsrc, w_all.at[:, z // CORES], w_snd.at[d - 1], w_rcv.at[z // CORES],
            dev(x, c, y, (z + d) % Z),
        )

    @pl.when(mine)
    def _():
        pltpu.make_async_copy(wsrc, w_all.at[:, z // CORES], w_rcv.at[z // CORES]).start()
        for d in range(1, Z):
            @pl.when(z + d >= Z)
            def _():
                weight_to(d).start()

    go(remote(
        act_send.at[pl.ds((1 - c) * Y, Y)], act_mid, a_snd.at[0], a_rcv.at[0], sister
    ))
    for k in range(PER):
        go(cot_to(k, None, sister, sis_send.at[k, 0]))
    for dy in range(1, Y):
        go(blocks_to(dy, act_send.at[c * Y + (y + dy) % Y], c, dy))
    act_all[pl.ds(lead + PER * c, PER), y] = act_send[c * Y + y]
    mid = remote(act_mid, act_mid, a_snd.at[0], a_rcv.at[0], sister)
    mid.wait_recv()
    for dy in range(1, Y):
        go(blocks_to(Y - 1 + dy, act_mid.at[(y + dy) % Y], 1 - c, dy))
    for k in range(PER):
        ends = (up, down) if k == 0 else (down, up)
        for n, row in enumerate(ends):
            go(cot_to(k, None, dev(x, c, row, z), own_send.at[k, n]))
    act_all[pl.ds(lead + PER * (1 - c), PER), y] = act_mid[y]

    def clear(s, _):
        grad[s] = jnp.zeros(grad.shape[1:], F32)
        return 0

    def clear_edges(s, _):
        for edge in (0, Y + 1):
            lhs[s, edge] = jnp.zeros(lhs.shape[2:], BF16)
        return 0

    lax.fori_loop(0, span, clear, 0)
    lax.fori_loop(0, span + lead, clear_edges, 0)
    total[...] = jnp.zeros(total.shape, F32)

    for k in range(PER):
        arrived(PER * c + k, y)

    def halo_late(row, slot):
        @pl.when(c == 1)
        def _():
            arrived(1, row)
            halo_to(row, slot).start()

    @pl.when(c == 0)
    def _():
        halo_to(y, 0).start()

    halo_late(y, 0)
    for dy in range(1, Y):
        for n, core in ((dy, c), (Y - 1 + dy, 1 - c)):
            blocks = act_all.at[pl.ds(lead + PER * core, PER), (y + Y - dy) % Y]
            remote(blocks, blocks, a_snd.at[n], a_rcv.at[n], sister).wait_recv()
    go(remote(
        act_all.at[pl.ds(span, lead)], act_all.at[pl.ds(0, lead)], p_snd, p_rcv, dev(next_x, c, y, z)
    ))

    i = lax.broadcasted_iota(jnp.int32, (chunk, 1), 0)
    channel = (i // Z) * half + c * per_core + y * Z + i % Z
    groups = centre.shape[1]
    group = (i // Z) * (groups // X) + c * (groups // X // CORES) + y

    def column(row, index):
        lane = lax.broadcasted_iota(jnp.int32, (chunk, row.shape[1]), 1)
        return jnp.sum(jnp.where(lane == index, row, 0.0), axis=1, keepdims=True)

    mean, scale = column(centre[...], group), column(spread[...], group)
    gains, biases = column(gain[...], channel), column(bias[...], channel)
    clip_len = clip_frames[0]

    def valid(f):
        t = x * span + f
        return jnp.where((t >= 0) & (t < clip_len), 1.0, 0.0).astype(F32)

    lane = lax.broadcasted_iota(jnp.int32, (chunk, cols), 1)

    def block_input(s, r):
        norm = (act_all[s + lead, r].astype(F32) - mean) * scale
        shifted = norm * gains + biases
        sig = jax.nn.sigmoid(shifted)
        a = shifted * sig * valid(s)
        at = s + lead
        lhs[at, r + 1, pl.ds(0, chunk)] = jnp.where(lane == 0, 0.0, pltpu.roll(a, 1, 1)).astype(BF16)
        lhs[at, r + 1, pl.ds(chunk, chunk)] = a.astype(BF16)
        lhs[at, r + 1, pl.ds(2 * chunk, chunk)] = jnp.where(
            lane == cols - 1, 0.0, pltpu.roll(a, cols - 1, 1)
        ).astype(BF16)
        return norm, shifted, sig

    def prepare(t, _):
        s, r = t // Y, t % Y
        norm, shifted, sig = block_input(s, r)
        normed[s, r] = norm
        slope[s, r] = sig * (1.0 + shifted * (1.0 - sig)) * valid(s) * gains
        return 0

    def prepare_before(t, _):
        block_input(t // Y - lead, t % Y)
        return 0

    lax.fori_loop(0, span * Y, prepare, 0, unroll=2)

    rows3 = lhs.shape[2]

    def masked(f, r):
        return jnp.where(x * span + f < clip_len, cots[f, r], jnp.zeros((cols, ch), BF16))

    def weight_row(r):
        for f in range(span):
            @pl.when((c != f // PER) & ((c == 0) | (f != 1)))
            def _():
                arrived(f, r)

        left = [lhs[pl.ds(f, 3), pl.ds(r, 3)].reshape(9 * rows3, cols) for f in range(span)]
        right = [masked(f, r) for f in range(span)]
        term = nn(jnp.concatenate(left, axis=1), jnp.concatenate(right, axis=0))
        total[...] += term.reshape(27, chunk, ch)

    parts = [(t, min(8, 27 - t)) for t in range(0, 27, 8)]

    def sent_rows(taps):
        return -(-taps * Z // 16) * 16

    def reduce_x(j):
        tap, taps = parts[j]
        rows, whole = taps * Z, sent_rows(taps)
        for xx in range(X):
            x_send[j, xx, pl.ds(0, rows)] = (
                total[pl.ds(tap, taps), pl.ds(xx * Z, Z)].reshape(rows, ch).astype(BF16)
            )
            if whole > rows:
                x_send[j, xx, pl.ds(rows, whole - rows)] = jnp.zeros((whole - rows, ch), BF16)
        for d in range(1, X):
            xx = (x + d) % X
            go(remote(
                x_send.at[j, xx, pl.ds(0, whole)], x_recv.at[j, d - 1, pl.ds(0, whole)],
                x_snd.at[j, d - 1], x_rcv.at[j, d - 1], dev(xx, c, y, z),
            ))

    def reduce_z(j):
        tap, taps = parts[j]
        rows, whole = taps * Z, sent_rows(taps)
        for d in range(1, X):
            got = x_recv.at[j, d - 1, pl.ds(0, whole)]
            pltpu.make_async_copy(got, got, x_rcv.at[j, d - 1]).wait()
        part = total[pl.ds(tap, taps), pl.ds(x * Z, Z)].reshape(rows, ch)
        for d in range(1, X):
            part = part + x_recv[j, d - 1, pl.ds(0, rows)].astype(F32)
        for h in range(halves):
            row_sum[h, pl.ds(0, rows)] = part[:, h * 128 : (h + 1) * 128]
        for zz in range(Z):
            for h in range(halves):
                z_send[j, zz, :, pl.ds(h * 128, 128)] = row_sum[h, pl.ds(zz, 8, Z), :]
        for d in range(1, Z):
            zz = (z + d) % Z
            go(remote(
                z_send.at[j, zz], z_recv.at[j, d - 1], z_snd.at[j, d - 1], z_rcv.at[j, d - 1],
                dev(x, c, y, zz),
            ))


    across = (y + 2) % Y
    seen = [1, 1]

    def take(k, row, on):
        arrived(PER * c + k, row)
        if on is not None:
            go(cot_to(k, row, dev(x, c, on, z), fwd_send.at[k]))
        n = seen[k]
        seen[k] += 1
        go(cot_to(k, row, sister, sis_send.at[k, n]))

        if k == 0:
            @pl.when(c == 0)
            def _():
                halo_to(row, n).start()

    take(0, down, up)
    take(0, up, None)

    @pl.when(z < Z - 1)
    def _():
        pl.semaphore_wait(z_ready, Z - 1 - z)

    @pl.when(mine)
    def _():
        for d in range(1, Z):
            @pl.when(z + d < Z)
            def _():
                weight_to(d).start()

    pltpu.make_async_copy(act_all.at[pl.ds(0, lead)], act_all.at[pl.ds(0, lead)], p_rcv).wait()
    lax.fori_loop(0, lead * Y, prepare_before, 0, unroll=2)
    take(1, up, down)
    take(1, down, None)
    halo_late(down, 1)
    halo_late(up, 2)

    def turn(n):
        return (y + n + (n // 2) * (1 - 2 * (n % 2))) % Y

    def early(n, _):
        weight_row(turn(n))
        return 0

    lax.fori_loop(0, Y - 1, early, 0)

    def halo_on(d):
        r = (y + d) % Y
        arrived(span + c, r)
        go(remote(
            cots.at[span + c, r], cots.at[span + c, r], fwd_send.at[PER + d], cot_sem.at[span + c, r],
            sister,
        ))

    halo_on(0)
    take(0, across, None)
    take(1, across, None)
    halo_late(across, 3)
    weight_row(across)
    row_sum[...] = jnp.zeros(row_sum.shape, F32)
    for j in range(len(parts)):
        reduce_x(j)

    for n in range(X):
        pltpu.make_async_copy(w_all.at[:, n], w_all.at[:, n], w_rcv.at[n]).wait()

    for k in range(9):
        tap = w_all[pl.ds(3 * k, 3)].astype(F32).reshape(rows3, ch)
        w_taps[pl.ds(k % 3 * rows3, rows3), pl.ds((2 - k // 3) * ch, ch)] = tap.astype(BF16)

    def input_term(s, f0, f1, r):
        k0, k1 = (f0 - s) * ch, (f1 - s) * ch
        right = jnp.concatenate([masked(f, r) for f in range(f0, f1)], axis=1)
        part = nt(w_taps[:, pl.ds(k0, k1 - k0)], right)
        grad[s, pl.ds(r, 3)] += part.reshape(3, rows3, cols)

    def input_rows(n, _):
        for s in range(span):
            input_term(s, s, min(s + 3, span), turn(n))
        return 0

    def halo_input(d):
        r = (y + d) % Y
        for f in range(span, span + lead):
            @pl.when(c != f - span)
            def _():
                arrived(f, r)

        for s in range(span - lead, span):
            input_term(s, span, s + 3, r)

    lax.fori_loop(0, 2, input_rows, 0)
    halo_on(1)
    halo_on(3)
    lax.fori_loop(2, Y, input_rows, 0)

    def gather(t, carry):
        first, second = carry
        s, r = t // Y, t % Y
        g0 = grad[s, r + 1, pl.ds(0, chunk)]
        g1 = grad[s, r + 1, pl.ds(chunk, chunk)]
        g2 = grad[s, r + 1, pl.ds(2 * chunk, chunk)]
        whole = (
            jnp.where(lane == cols - 1, 0.0, pltpu.roll(g0, cols - 1, 1)) + g1
            + jnp.where(lane == 0, 0.0, pltpu.roll(g2, 1, 1))
        )
        upstream = whole * slope[s, r]
        slope[s, r] = upstream
        return first + upstream, second + upstream * normed[s, r]

    nothing = jnp.zeros((chunk, cols), F32)
    early_sums = lax.fori_loop(0, (span - lead) * Y, gather, (nothing, nothing), unroll=2)
    for d in (0, 1, 3):
        halo_input(d)
    reduce_z(0)
    halo_on(2)
    reduce_z(1)
    halo_input(2)
    first, second = lax.fori_loop((span - lead) * Y, span * Y, gather, early_sums, unroll=2)
    slim = lax.broadcasted_iota(jnp.int32, (chunk, 128), 1)
    first = jnp.sum(first, axis=1, keepdims=True)
    second = jnp.sum(second, axis=1, keepdims=True)
    s_send[...] = jnp.where(slim == 0, first, jnp.where(slim == 1, second, 0.0))
    for d in range(1, X):
        go(remote(
            s_send, s_recv.at[d - 1], s_snd.at[d - 1], s_rcv.at[d - 1], dev((x + d) % X, c, y, z)
        ))

    reduce_z(2)
    reduce_z(3)

    for d in range(1, X):
        pltpu.make_async_copy(s_recv.at[d - 1], s_recv.at[d - 1], s_rcv.at[d - 1]).wait()
    both = s_send[...]
    for d in range(1, X):
        both = both + s_recv[d - 1]
    both = both.reshape(X, Z, 128)
    both = jnp.broadcast_to(jnp.sum(both, axis=1, keepdims=True), (X, Z, 128)).reshape(chunk, 128)
    population = clip_len.astype(F32) * (Y * cols * Z)
    first = jnp.sum(jnp.where(slim == 0, both, 0.0), axis=1, keepdims=True) / population
    second = jnp.sum(jnp.where(slim == 1, both, 0.0), axis=1, keepdims=True) / population

    def finish(core):
        def body(t, _):
            s, r = PER * core + t // Y, t % Y
            value = scale * (slope[s, r] - first - normed[s, r] * second) * valid(s)
            g_send[s, r] = value.astype(BF16)
            return 0

        lax.fori_loop(0, PER * Y, body, 0, unroll=4)

    finish(1 - c)
    go(remote(g_send.at[pl.ds(PER * (1 - c), PER)], g_mid, g_snd.at[0], g_rcv.at[0], sister))
    finish(c)

    def rows_to(n, src, core, dy):
        return remote(
            src, g_recv.at[core * Y + y], g_snd.at[n], g_rcv.at[n], dev(x, c, (y + dy) % Y, z)
        )

    for dy in range(1, Y):
        go(rows_to(dy, g_send.at[pl.ds(PER * c, PER), (y + dy) % Y], c, dy))
    g_recv[c * Y + y] = g_send[pl.ds(PER * c, PER), y]
    remote(g_mid, g_mid, g_snd.at[0], g_rcv.at[0], sister).wait_recv()
    for dy in range(1, Y):
        go(rows_to(Y - 1 + dy, g_mid.at[:, (y + dy) % Y], 1 - c, dy))
    g_recv[(1 - c) * Y + y] = g_mid[:, y]

    final = z_send[:, z]
    for j in range(len(parts)):
        for d in range(1, Z):
            pltpu.make_async_copy(z_recv.at[j, d - 1], z_recv.at[j, d - 1], z_rcv.at[j, d - 1]).wait()
    for d in range(1, Z):
        final = final + z_recv[:, d - 1]
    final = final.reshape(len(parts) * 8, ch)[:27]
    cells = X * Y * Z * CORES * PER * cols
    wout[...] = (final * (1.0 / cells)).astype(BF16)

    for dy in range(1, Y):
        for n, core in ((dy, c), (Y - 1 + dy, 1 - c)):
            rows = g_recv.at[core * Y + (y + Y - dy) % Y]
            remote(rows, rows, g_snd.at[n], g_rcv.at[n], sister).wait_recv()
    for k in range(PER):
        out[k] = tn(g_recv[:, k].reshape(ch, cols), pick).astype(BF16)

    for copy in sends:
        copy.wait_send()

    for n in range(Y):
        halo_to(y, n).wait_send()

    @pl.when(mine)
    def _():
        for d in range(1, Z):
            weight_to(d).wait_send()


def per_device(X, Y, Z, acts, cot, clip_frames, weight, centre, spread, gain, bias):
    _, per, _, cols, ch = acts.shape
    span, lead = CORES * per, 2
    chunk = ch // (CORES * Y)
    taps = weight.shape[1]
    dma = pltpu.SemaphoreType.DMA
    hbm = pl.BlockSpec(memory_space=pl.ANY)
    vmem = pl.BlockSpec(memory_space=pltpu.VMEM)
    grad_input, weight_grad = pl.pallas_call(
        functools.partial(fused, X, Y, Z),
        out_shape=(
            jax.ShapeDtypeStruct((per, cols, ch), BF16),
            jax.ShapeDtypeStruct((taps, ch), BF16),
        ),
        in_specs=[pl.BlockSpec(memory_space=pltpu.SMEM), hbm, hbm, hbm, vmem, vmem, vmem, vmem],
        out_specs=(vmem, vmem),
        scratch_shapes=[
            pltpu.VMEM((per, cols, ch), BF16),
            pltpu.VMEM((CORES * Y, per, chunk, cols), BF16),
            pltpu.VMEM((Y, per, chunk, cols), BF16),
            pltpu.VMEM((span + lead, Y, chunk, cols), BF16),
            pltpu.VMEM((span + lead, Y, cols, ch), BF16),
            pltpu.VMEM((taps, X, Z, ch), BF16),
            pltpu.VMEM((9 * chunk, 3 * ch), BF16),
            pltpu.VMEM((span + lead, Y + 2, 3 * chunk, cols), BF16),
            pltpu.VMEM((span, Y + 2, 3 * chunk, cols), F32),
            pltpu.VMEM((span, Y, chunk, cols), F32),
            pltpu.VMEM((span, Y, chunk, cols), F32),
            pltpu.VMEM((taps, chunk, ch), F32),
            pltpu.VMEM((4, X, 8 * Z, ch), BF16),
            pltpu.VMEM((4, X - 1, 8 * Z, ch), BF16),
            pltpu.VMEM((ch // 128, 8 * Z, 128), F32),
            pltpu.VMEM((4, Z, 8, ch), F32),
            pltpu.VMEM((4, Z - 1, 8, ch), F32),
            pltpu.VMEM((chunk, 128), F32),
            pltpu.VMEM((X - 1, chunk, 128), F32),
            pltpu.VMEM((span, Y, chunk, cols), BF16),
            pltpu.VMEM((per, Y, chunk, cols), BF16),
            pltpu.VMEM((CORES * Y, per, chunk, cols), BF16),
            dma,
            dma((span + lead, Y)),
            dma((per, 2)),
            dma((per + Y,)),
            dma((per, Y)),
            dma((Y,)),
            dma((CORES * Y - 1,)),
            dma((CORES * Y - 1,)),
            dma((Z - 1,)),
            dma((X,)),
            dma((4, X - 1)),
            dma((4, X - 1)),
            dma((4, Z - 1)),
            dma((4, Z - 1)),
            dma((X - 1,)),
            dma((X - 1,)),
            dma((CORES * Y - 1,)),
            dma((CORES * Y - 1,)),
            dma,
            dma,
            pltpu.SemaphoreType.REGULAR,
        ],
        compiler_params=pltpu.CompilerParams(
            collective_id=0, has_side_effects=True, vmem_limit_bytes=60 * 1024 * 1024
        ),
    )(
        clip_frames,
        acts.reshape(per, cols, ch),
        cot.reshape(per, cols, ch),
        weight.transpose(1, 0, 2).reshape(taps, Y, Z, ch),
        centre,
        spread,
        gain.reshape(1, ch),
        bias.reshape(1, ch),
    )
    return grad_input.reshape(1, per, 1, cols, ch), weight_grad


def solution(mesh):
    X, Y, Z = mesh.shape["tm"] // CORES, mesh.shape["height"], mesh.shape["dp"]
    return jax.shard_map(
        functools.partial(per_device, X, Y, Z),
        mesh=mesh,
        in_specs=(
            P("dp", "tm", "height", None, None),
            P("dp", "tm", "height", None, None),
            P("dp"),
            P("dp", None, None),
            P("dp", None),
            P("dp", None),
            P(),
            P(),
        ),
        out_specs=(P("dp", "tm", "height", None, None), P(("tm", "height", "dp"), None)),
        check_vma=False,
    )
```

```python
import functools

import jax
import jax.numpy as jnp
from jax import lax
from jax.experimental import pallas as pl
from jax.experimental.pallas import tpu as pltpu
from jax.sharding import PartitionSpec as P

CORES = 2
PER = 2
MESH = pl.DeviceIdType.MESH
F32 = jnp.float32
BF16 = jnp.bfloat16


def nt(a, b):
    return lax.dot_general(a, b, (((1,), (1,)), ((), ())), preferred_element_type=F32)


def nn(a, b):
    return lax.dot_general(a, b, (((1,), (0,)), ((), ())), preferred_element_type=F32)


def tn(a, b):
    return lax.dot_general(a, b, (((0,), (0,)), ((), ())), preferred_element_type=F32)


def fused(
    X, Y, Z,
    clip_frames, acts, cot, weight, centre, spread, gain, bias,
    out, wout,
    act_in, act_send, act_mid, act_all, cots, w_all, w_taps, lhs, grad, normed, slope,
    total, x_send, x_recv, row_sum, z_send, z_recv, s_send, s_recv, g_send, g_mid, g_recv,
    act_sem, cot_sem, own_send, fwd_send, sis_send, halo_send, a_snd, a_rcv, w_snd, w_rcv,
    x_snd, x_rcv, z_snd, z_rcv, s_snd, s_rcv, g_snd, g_rcv, p_snd, p_rcv, z_ready,
):
    tm = lax.axis_index("tm")
    y = lax.axis_index("height")
    z = lax.axis_index("dp")
    x = tm // CORES
    c = tm % CORES
    span = CORES * PER
    cols, ch = cots.shape[2], cots.shape[3]
    chunk = act_all.shape[2]
    lead = 2
    halves = ch // 128

    def dev(xx, cc, yy, zz):
        return (xx * CORES + cc, yy, zz)

    def remote(src, dst, snd, rcv, target):
        return pltpu.make_async_remote_copy(
            src_ref=src, dst_ref=dst, send_sem=snd, recv_sem=rcv,
            device_id=target, device_id_type=MESH,
        )

    up, down = (y + 1) % Y, (y + Y - 1) % Y
    prev_x, next_x = (x + X - 1) % X, (x + 1) % X
    sister = dev(x, 1 - c, y, z)

    act_copy = pltpu.make_async_copy(acts, act_in, act_sem)
    act_copy.start()
    for k in range(PER):
        pltpu.make_async_copy(cot.at[k], cots.at[PER * c + k, y], cot_sem.at[PER * c + k, y]).start()

    barrier = pltpu.get_barrier_semaphore()
    partners = [sister] + [dev(x, c, (y + dy) % Y, z) for dy in range(1, Y)]
    partners += [dev((x + dx) % X, c, y, z) for dx in range(1, X)]
    for target in partners:
        pl.semaphore_signal(barrier, inc=1, device_id=target, device_id_type=MESH)

    for d in range(1, Z):
        @pl.when(z + d < Z)
        def _():
            pl.semaphore_signal(
                barrier, inc=1, device_id=dev(x, c, y, (z + d) % Z), device_id_type=MESH
            )

    row_id = lax.broadcasted_iota(jnp.int32, (ch, ch), 0)
    col_id = lax.broadcasted_iota(jnp.int32, (ch, ch), 1)
    half = ch // X
    per_core = half // CORES
    order = (
        ((row_id // Z) % X) * half + (row_id // (chunk * Y)) * per_core
        + ((row_id // chunk) % Y) * Z + row_id % Z
    )
    pick = jnp.where(order == col_id, 1.0, 0.0).astype(BF16)
    act_copy.wait()
    for k in range(PER):
        act_send[:, k] = nt(pick, act_in[k]).astype(BF16).reshape(CORES * Y, chunk, cols)

    pl.semaphore_wait(barrier, len(partners) + z)

    def cot_to(k, row, target, snd):
        src = cot.at[k] if row is None else cots.at[PER * c + k, row]
        at = y if row is None else row
        return remote(src, cots.at[PER * c + k, at], snd, cot_sem.at[PER * c + k, at], target)

    def halo_to(row, slot):
        return remote(
            cots.at[c, row], cots.at[span + c, row], halo_send.at[slot], cot_sem.at[span + c, row],
            dev(prev_x, c, y, z),
        )

    sends = []

    def go(copy):
        copy.start()
        sends.append(copy)

    def arrived(f, row):
        remote(
            cots.at[f, row], cots.at[f, row], own_send.at[0, 0], cot_sem.at[f, row], sister
        ).wait_recv()

    def blocks_to(n, src, core, dy):
        return remote(
            src, act_all.at[pl.ds(lead + PER * core, PER), y], a_snd.at[n], a_rcv.at[n],
            dev(x, c, (y + dy) % Y, z),
        )

    for d in range(1, Z):
        @pl.when(z >= d)
        def _():
            pl.semaphore_signal(
                z_ready, inc=1, device_id=dev(x, c, y, (z + Z - d) % Z), device_id_type=MESH
            )

    mine = (z % CORES) == c
    wsrc = weight.at[:, y]

    def weight_to(d):
        return remote(
            wsrc, w_all.at[:, z // CORES], w_snd.at[d - 1], w_rcv.at[z // CORES],
            dev(x, c, y, (z + d) % Z),
        )

    @pl.when(mine)
    def _():
        pltpu.make_async_copy(wsrc, w_all.at[:, z // CORES], w_rcv.at[z // CORES]).start()
        for d in range(1, Z):
            @pl.when(z + d >= Z)
            def _():
                weight_to(d).start()

    go(remote(
        act_send.at[pl.ds((1 - c) * Y, Y)], act_mid, a_snd.at[0], a_rcv.at[0], sister
    ))
    for k in range(PER):
        go(cot_to(k, None, sister, sis_send.at[k, 0]))
    for dy in range(1, Y):
        go(blocks_to(dy, act_send.at[c * Y + (y + dy) % Y], c, dy))
    act_all[pl.ds(lead + PER * c, PER), y] = act_send[c * Y + y]
    mid = remote(act_mid, act_mid, a_snd.at[0], a_rcv.at[0], sister)
    mid.wait_recv()
    for dy in range(1, Y):
        go(blocks_to(Y - 1 + dy, act_mid.at[(y + dy) % Y], 1 - c, dy))
    for k in range(PER):
        ends = (up, down) if k == 0 else (down, up)
        for n, row in enumerate(ends):
            go(cot_to(k, None, dev(x, c, row, z), own_send.at[k, n]))
    act_all[pl.ds(lead + PER * (1 - c), PER), y] = act_mid[y]

    def clear(s, _):
        grad[s] = jnp.zeros(grad.shape[1:], F32)
        return 0

    def clear_edges(s, _):
        for edge in (0, Y + 1):
            lhs[s, edge] = jnp.zeros(lhs.shape[2:], BF16)
        return 0

    lax.fori_loop(0, span, clear, 0)
    lax.fori_loop(0, span + lead, clear_edges, 0)
    total[...] = jnp.zeros(total.shape, F32)

    for k in range(PER):
        arrived(PER * c + k, y)

    def halo_late(row, slot):
        @pl.when(c == 1)
        def _():
            arrived(1, row)
            halo_to(row, slot).start()

    @pl.when(c == 0)
    def _():
        halo_to(y, 0).start()

    halo_late(y, 0)
    for dy in range(1, Y):
        for n, core in ((dy, c), (Y - 1 + dy, 1 - c)):
            blocks = act_all.at[pl.ds(lead + PER * core, PER), (y + Y - dy) % Y]
            remote(blocks, blocks, a_snd.at[n], a_rcv.at[n], sister).wait_recv()
    go(remote(
        act_all.at[pl.ds(span, lead)], act_all.at[pl.ds(0, lead)], p_snd, p_rcv, dev(next_x, c, y, z)
    ))

    i = lax.broadcasted_iota(jnp.int32, (chunk, 1), 0)
    channel = (i // Z) * half + c * per_core + y * Z + i % Z
    groups = centre.shape[1]
    group = (i // Z) * (groups // X) + c * (groups // X // CORES) + y

    def column(row, index):
        lane = lax.broadcasted_iota(jnp.int32, (chunk, row.shape[1]), 1)
        return jnp.sum(jnp.where(lane == index, row, 0.0), axis=1, keepdims=True)

    mean, scale = column(centre[...], group), column(spread[...], group)
    gains, biases = column(gain[...], channel), column(bias[...], channel)
    clip_len = clip_frames[0]

    def valid(f):
        t = x * span + f
        return jnp.where((t >= 0) & (t < clip_len), 1.0, 0.0).astype(F32)

    lane = lax.broadcasted_iota(jnp.int32, (chunk, cols), 1)

    def block_input(s, r):
        norm = (act_all[s + lead, r].astype(F32) - mean) * scale
        shifted = norm * gains + biases
        sig = jax.nn.sigmoid(shifted)
        a = shifted * sig * valid(s)
        at = s + lead
        lhs[at, r + 1, pl.ds(0, chunk)] = jnp.where(lane == 0, 0.0, pltpu.roll(a, 1, 1)).astype(BF16)
        lhs[at, r + 1, pl.ds(chunk, chunk)] = a.astype(BF16)
        lhs[at, r + 1, pl.ds(2 * chunk, chunk)] = jnp.where(
            lane == cols - 1, 0.0, pltpu.roll(a, cols - 1, 1)
        ).astype(BF16)
        return norm, shifted, sig

    def prepare(t, _):
        s, r = t // Y, t % Y
        norm, shifted, sig = block_input(s, r)
        normed[s, r] = norm
        slope[s, r] = sig * (1.0 + shifted * (1.0 - sig)) * valid(s) * gains
        return 0

    def prepare_before(t, _):
        block_input(t // Y - lead, t % Y)
        return 0

    lax.fori_loop(0, span * Y, prepare, 0, unroll=2)

    rows3 = lhs.shape[2]

    def masked(f, r):
        return jnp.where(x * span + f < clip_len, cots[f, r], jnp.zeros((cols, ch), BF16))

    def weight_row(r):
        for f in range(span):
            @pl.when((c != f // PER) & ((c == 0) | (f != 1)))
            def _():
                arrived(f, r)

        left = [lhs[pl.ds(f, 3), pl.ds(r, 3)].reshape(9 * rows3, cols) for f in range(span)]
        right = [masked(f, r) for f in range(span)]
        term = nn(jnp.concatenate(left, axis=1), jnp.concatenate(right, axis=0))
        total[...] += term.reshape(27, chunk, ch)

    parts = [(t, min(8, 27 - t)) for t in range(0, 27, 8)]

    def sent_rows(taps):
        return -(-taps * Z // 16) * 16

    def reduce_x(j):
        tap, taps = parts[j]
        rows, whole = taps * Z, sent_rows(taps)
        for xx in range(X):
            x_send[j, xx, pl.ds(0, rows)] = (
                total[pl.ds(tap, taps), pl.ds(xx * Z, Z)].reshape(rows, ch).astype(BF16)
            )
            if whole > rows:
                x_send[j, xx, pl.ds(rows, whole - rows)] = jnp.zeros((whole - rows, ch), BF16)
        for d in range(1, X):
            xx = (x + d) % X
            go(remote(
                x_send.at[j, xx, pl.ds(0, whole)], x_recv.at[j, d - 1, pl.ds(0, whole)],
                x_snd.at[j, d - 1], x_rcv.at[j, d - 1], dev(xx, c, y, z),
            ))

    def reduce_z(j):
        tap, taps = parts[j]
        rows, whole = taps * Z, sent_rows(taps)
        for d in range(1, X):
            got = x_recv.at[j, d - 1, pl.ds(0, whole)]
            pltpu.make_async_copy(got, got, x_rcv.at[j, d - 1]).wait()
        part = total[pl.ds(tap, taps), pl.ds(x * Z, Z)].reshape(rows, ch)
        for d in range(1, X):
            part = part + x_recv[j, d - 1, pl.ds(0, rows)].astype(F32)
        for h in range(halves):
            row_sum[h, pl.ds(0, rows)] = part[:, h * 128 : (h + 1) * 128]
        for zz in range(Z):
            for h in range(halves):
                z_send[j, zz, :, pl.ds(h * 128, 128)] = row_sum[h, pl.ds(zz, 8, Z), :]
        for d in range(1, Z):
            zz = (z + d) % Z
            go(remote(
                z_send.at[j, zz], z_recv.at[j, d - 1], z_snd.at[j, d - 1], z_rcv.at[j, d - 1],
                dev(x, c, y, zz),
            ))


    across = (y + 2) % Y
    seen = [1, 1]

    def take(k, row, on):
        arrived(PER * c + k, row)
        if on is not None:
            go(cot_to(k, row, dev(x, c, on, z), fwd_send.at[k]))
        n = seen[k]
        seen[k] += 1
        go(cot_to(k, row, sister, sis_send.at[k, n]))

        if k == 0:
            @pl.when(c == 0)
            def _():
                halo_to(row, n).start()

    take(0, down, up)
    take(0, up, None)

    @pl.when(z < Z - 1)
    def _():
        pl.semaphore_wait(z_ready, Z - 1 - z)

    @pl.when(mine)
    def _():
        for d in range(1, Z):
            @pl.when(z + d < Z)
            def _():
                weight_to(d).start()

    pltpu.make_async_copy(act_all.at[pl.ds(0, lead)], act_all.at[pl.ds(0, lead)], p_rcv).wait()
    lax.fori_loop(0, lead * Y, prepare_before, 0, unroll=2)
    take(1, up, down)
    take(1, down, None)
    halo_late(down, 1)
    halo_late(up, 2)

    def turn(n):
        return (y + n + (n // 2) * (1 - 2 * (n % 2))) % Y

    def early(n, _):
        weight_row(turn(n))
        return 0

    lax.fori_loop(0, Y - 1, early, 0)

    def halo_on(d):
        r = (y + d) % Y
        arrived(span + c, r)
        go(remote(
            cots.at[span + c, r], cots.at[span + c, r], fwd_send.at[PER + d], cot_sem.at[span + c, r],
            sister,
        ))

    halo_on(0)
    take(0, across, None)
    take(1, across, None)
    halo_late(across, 3)
    weight_row(across)
    row_sum[...] = jnp.zeros(row_sum.shape, F32)
    for j in range(len(parts)):
        reduce_x(j)

    for n in range(X):
        pltpu.make_async_copy(w_all.at[:, n], w_all.at[:, n], w_rcv.at[n]).wait()

    for k in range(9):
        tap = w_all[pl.ds(3 * k, 3)].astype(F32).reshape(rows3, ch)
        w_taps[pl.ds(k % 3 * rows3, rows3), pl.ds((2 - k // 3) * ch, ch)] = tap.astype(BF16)

    def input_term(s, f0, f1, r):
        k0, k1 = (f0 - s) * ch, (f1 - s) * ch
        right = jnp.concatenate([masked(f, r) for f in range(f0, f1)], axis=1)
        part = nt(w_taps[:, pl.ds(k0, k1 - k0)], right)
        grad[s, pl.ds(r, 3)] += part.reshape(3, rows3, cols)

    def input_rows(n, _):
        for s in range(span):
            input_term(s, s, min(s + 3, span), turn(n))
        return 0

    def halo_input(d):
        r = (y + d) % Y
        for f in range(span, span + lead):
            @pl.when(c != f - span)
            def _():
                arrived(f, r)

        for s in range(span - lead, span):
            input_term(s, span, s + 3, r)

    lax.fori_loop(0, 2, input_rows, 0)
    halo_on(1)
    halo_on(3)
    lax.fori_loop(2, Y, input_rows, 0)

    def gather(t, carry):
        first, second = carry
        s, r = t // Y, t % Y
        g0 = grad[s, r + 1, pl.ds(0, chunk)]
        g1 = grad[s, r + 1, pl.ds(chunk, chunk)]
        g2 = grad[s, r + 1, pl.ds(2 * chunk, chunk)]
        whole = (
            jnp.where(lane == cols - 1, 0.0, pltpu.roll(g0, cols - 1, 1)) + g1
            + jnp.where(lane == 0, 0.0, pltpu.roll(g2, 1, 1))
        )
        upstream = whole * slope[s, r]
        slope[s, r] = upstream
        return first + upstream, second + upstream * normed[s, r]

    nothing = jnp.zeros((chunk, cols), F32)
    early_sums = lax.fori_loop(0, (span - lead) * Y, gather, (nothing, nothing), unroll=2)
    for d in (0, 1, 3):
        halo_input(d)
    reduce_z(0)
    halo_on(2)
    reduce_z(1)
    halo_input(2)
    first, second = lax.fori_loop((span - lead) * Y, span * Y, gather, early_sums, unroll=2)
    slim = lax.broadcasted_iota(jnp.int32, (chunk, 128), 1)
    first = jnp.sum(first, axis=1, keepdims=True)
    second = jnp.sum(second, axis=1, keepdims=True)
    s_send[...] = jnp.where(slim == 0, first, jnp.where(slim == 1, second, 0.0))
    for d in range(1, X):
        go(remote(
            s_send, s_recv.at[d - 1], s_snd.at[d - 1], s_rcv.at[d - 1], dev((x + d) % X, c, y, z)
        ))

    reduce_z(2)
    reduce_z(3)

    for d in range(1, X):
        pltpu.make_async_copy(s_recv.at[d - 1], s_recv.at[d - 1], s_rcv.at[d - 1]).wait()
    both = s_send[...]
    for d in range(1, X):
        both = both + s_recv[d - 1]
    both = both.reshape(X, Z, 128)
    both = jnp.broadcast_to(jnp.sum(both, axis=1, keepdims=True), (X, Z, 128)).reshape(chunk, 128)
    population = clip_len.astype(F32) * (Y * cols * Z)
    first = jnp.sum(jnp.where(slim == 0, both, 0.0), axis=1, keepdims=True) / population
    second = jnp.sum(jnp.where(slim == 1, both, 0.0), axis=1, keepdims=True) / population

    def finish(core):
        def body(t, _):
            s, r = PER * core + t // Y, t % Y
            value = scale * (slope[s, r] - first - normed[s, r] * second) * valid(s)
            g_send[s, r] = value.astype(BF16)
            return 0

        lax.fori_loop(0, PER * Y, body, 0, unroll=4)

    finish(1 - c)
    go(remote(g_send.at[pl.ds(PER * (1 - c), PER)], g_mid, g_snd.at[0], g_rcv.at[0], sister))
    finish(c)

    def rows_to(n, src, core, dy):
        return remote(
            src, g_recv.at[core * Y + y], g_snd.at[n], g_rcv.at[n], dev(x, c, (y + dy) % Y, z)
        )

    for dy in range(1, Y):
        go(rows_to(dy, g_send.at[pl.ds(PER * c, PER), (y + dy) % Y], c, dy))
    g_recv[c * Y + y] = g_send[pl.ds(PER * c, PER), y]
    remote(g_mid, g_mid, g_snd.at[0], g_rcv.at[0], sister).wait_recv()
    for dy in range(1, Y):
        go(rows_to(Y - 1 + dy, g_mid.at[:, (y + dy) % Y], 1 - c, dy))
    g_recv[(1 - c) * Y + y] = g_mid[:, y]

    final = z_send[:, z]
    for j in range(len(parts)):
        for d in range(1, Z):
            pltpu.make_async_copy(z_recv.at[j, d - 1], z_recv.at[j, d - 1], z_rcv.at[j, d - 1]).wait()
    for d in range(1, Z):
        final = final + z_recv[:, d - 1]
    final = final.reshape(len(parts) * 8, ch)[:27]
    cells = X * Y * Z * CORES * PER * cols
    wout[...] = (final * (1.0 / cells)).astype(BF16)

    for dy in range(1, Y):
        for n, core in ((dy, c), (Y - 1 + dy, 1 - c)):
            rows = g_recv.at[core * Y + (y + Y - dy) % Y]
            remote(rows, rows, g_snd.at[n], g_rcv.at[n], sister).wait_recv()
    for k in range(PER):
        out[k] = tn(g_recv[:, k].reshape(ch, cols), pick).astype(BF16)

    for copy in sends:
        copy.wait_send()

    for n in range(Y):
        halo_to(y, n).wait_send()

    @pl.when(mine)
    def _():
        for d in range(1, Z):
            weight_to(d).wait_send()


def per_device(X, Y, Z, acts, cot, clip_frames, weight, centre, spread, gain, bias):
    _, per, _, cols, ch = acts.shape
    span, lead = CORES * per, 2
    chunk = ch // (CORES * Y)
    taps = weight.shape[1]
    dma = pltpu.SemaphoreType.DMA
    hbm = pl.BlockSpec(memory_space=pl.ANY)
    vmem = pl.BlockSpec(memory_space=pltpu.VMEM)
    grad_input, weight_grad = pl.pallas_call(
        functools.partial(fused, X, Y, Z),
        out_shape=(
            jax.ShapeDtypeStruct((per, cols, ch), BF16),
            jax.ShapeDtypeStruct((taps, ch), BF16),
        ),
        in_specs=[pl.BlockSpec(memory_space=pltpu.SMEM), hbm, hbm, hbm, vmem, vmem, vmem, vmem],
        out_specs=(vmem, vmem),
        scratch_shapes=[
            pltpu.VMEM((per, cols, ch), BF16),
            pltpu.VMEM((CORES * Y, per, chunk, cols), BF16),
            pltpu.VMEM((Y, per, chunk, cols), BF16),
            pltpu.VMEM((span + lead, Y, chunk, cols), BF16),
            pltpu.VMEM((span + lead, Y, cols, ch), BF16),
            pltpu.VMEM((taps, X, Z, ch), BF16),
            pltpu.VMEM((9 * chunk, 3 * ch), BF16),
            pltpu.VMEM((span + lead, Y + 2, 3 * chunk, cols), BF16),
            pltpu.VMEM((span, Y + 2, 3 * chunk, cols), F32),
            pltpu.VMEM((span, Y, chunk, cols), F32),
            pltpu.VMEM((span, Y, chunk, cols), F32),
            pltpu.VMEM((taps, chunk, ch), F32),
            pltpu.VMEM((4, X, 8 * Z, ch), BF16),
            pltpu.VMEM((4, X - 1, 8 * Z, ch), BF16),
            pltpu.VMEM((ch // 128, 8 * Z, 128), F32),
            pltpu.VMEM((4, Z, 8, ch), F32),
            pltpu.VMEM((4, Z - 1, 8, ch), F32),
            pltpu.VMEM((chunk, 128), F32),
            pltpu.VMEM((X - 1, chunk, 128), F32),
            pltpu.VMEM((span, Y, chunk, cols), BF16),
            pltpu.VMEM((per, Y, chunk, cols), BF16),
            pltpu.VMEM((CORES * Y, per, chunk, cols), BF16),
            dma,
            dma((span + lead, Y)),
            dma((per, 2)),
            dma((per + Y,)),
            dma((per, Y)),
            dma((Y,)),
            dma((CORES * Y - 1,)),
            dma((CORES * Y - 1,)),
            dma((Z - 1,)),
            dma((X,)),
            dma((4, X - 1)),
            dma((4, X - 1)),
            dma((4, Z - 1)),
            dma((4, Z - 1)),
            dma((X - 1,)),
            dma((X - 1,)),
            dma((CORES * Y - 1,)),
            dma((CORES * Y - 1,)),
            dma,
            dma,
            pltpu.SemaphoreType.REGULAR,
        ],
        compiler_params=pltpu.CompilerParams(
            collective_id=0, has_side_effects=True, vmem_limit_bytes=54784 * 1024
        ),
    )(
        clip_frames,
        acts.reshape(per, cols, ch),
        cot.reshape(per, cols, ch),
        weight.transpose(1, 0, 2).reshape(taps, Y, Z, ch),
        centre,
        spread,
        gain.reshape(1, ch),
        bias.reshape(1, ch),
    )
    return grad_input.reshape(1, per, 1, cols, ch), weight_grad


def solution(mesh):
    X, Y, Z = mesh.shape["tm"] // CORES, mesh.shape["height"], mesh.shape["dp"]
    return jax.shard_map(
        functools.partial(per_device, X, Y, Z),
        mesh=mesh,
        in_specs=(
            P("dp", "tm", "height", None, None),
            P("dp", "tm", "height", None, None),
            P("dp"),
            P("dp", None, None),
            P("dp", None),
            P("dp", None),
            P(),
            P(),
        ),
        out_specs=(P("dp", "tm", "height", None, None), P(("tm", "height", "dp"), None)),
        check_vma=False,
    )
```

```python
import functools

import jax
import jax.numpy as jnp
from jax import lax
from jax.experimental import pallas as pl
from jax.experimental.pallas import tpu as pltpu
from jax.sharding import PartitionSpec as P

CORES = 2
PER = 2
MESH = pl.DeviceIdType.MESH
F32 = jnp.float32
BF16 = jnp.bfloat16


def nt(a, b):
    return lax.dot_general(a, b, (((1,), (1,)), ((), ())), preferred_element_type=F32)


def nn(a, b):
    return lax.dot_general(a, b, (((1,), (0,)), ((), ())), preferred_element_type=F32)


def tn(a, b):
    return lax.dot_general(a, b, (((0,), (0,)), ((), ())), preferred_element_type=F32)


def fused(
    X, Y, Z,
    clip_frames, acts, cot, weight, centre, spread, gain, bias,
    out, wout,
    act_in, act_send, act_mid, act_all, cots, w_all, w_taps, lhs, grad, normed, slope,
    total, x_send, x_recv, row_sum, z_send, z_recv, s_send, s_recv, g_send, g_mid, g_recv,
    act_sem, cot_sem, own_send, fwd_send, sis_send, halo_send, a_snd, a_rcv, w_snd, w_rcv,
    x_snd, x_rcv, z_snd, z_rcv, s_snd, s_rcv, g_snd, g_rcv, p_snd, p_rcv, z_ready,
):
    tm = lax.axis_index("tm")
    y = lax.axis_index("height")
    z = lax.axis_index("dp")
    x = tm // CORES
    c = tm % CORES
    span = CORES * PER
    cols, ch = cots.shape[2], cots.shape[3]
    chunk = act_all.shape[2]
    lead = 2
    halves = ch // 128

    def dev(xx, cc, yy, zz):
        return (xx * CORES + cc, yy, zz)

    def remote(src, dst, snd, rcv, target):
        return pltpu.make_async_remote_copy(
            src_ref=src, dst_ref=dst, send_sem=snd, recv_sem=rcv,
            device_id=target, device_id_type=MESH,
        )

    up, down = (y + 1) % Y, (y + Y - 1) % Y
    prev_x, next_x = (x + X - 1) % X, (x + 1) % X
    sister = dev(x, 1 - c, y, z)

    act_copy = pltpu.make_async_copy(acts, act_in, act_sem)
    act_copy.start()
    for k in range(PER):
        pltpu.make_async_copy(cot.at[k], cots.at[PER * c + k, y], cot_sem.at[PER * c + k, y]).start()

    barrier = pltpu.get_barrier_semaphore()
    partners = [sister] + [dev(x, c, (y + dy) % Y, z) for dy in range(1, Y)]
    partners += [dev((x + dx) % X, c, y, z) for dx in range(1, X)]
    for target in partners:
        pl.semaphore_signal(barrier, inc=1, device_id=target, device_id_type=MESH)

    for d in range(1, Z):
        @pl.when(z + d < Z)
        def _():
            pl.semaphore_signal(
                barrier, inc=1, device_id=dev(x, c, y, (z + d) % Z), device_id_type=MESH
            )

    row_id = lax.broadcasted_iota(jnp.int32, (ch, ch), 0)
    col_id = lax.broadcasted_iota(jnp.int32, (ch, ch), 1)
    half = ch // X
    per_core = half // CORES
    order = (
        ((row_id // Z) % X) * half + (row_id // (chunk * Y)) * per_core
        + ((row_id // chunk) % Y) * Z + row_id % Z
    )
    pick = jnp.where(order == col_id, 1.0, 0.0).astype(BF16)
    act_copy.wait()
    for k in range(PER):
        act_send[:, k] = nt(pick, act_in[k]).astype(BF16).reshape(CORES * Y, chunk, cols)

    pl.semaphore_wait(barrier, len(partners) + z)

    def cot_to(k, row, target, snd):
        src = cot.at[k] if row is None else cots.at[PER * c + k, row]
        at = y if row is None else row
        return remote(src, cots.at[PER * c + k, at], snd, cot_sem.at[PER * c + k, at], target)

    def halo_to(row, slot):
        return remote(
            cots.at[c, row], cots.at[span + c, row], halo_send.at[slot], cot_sem.at[span + c, row],
            dev(prev_x, c, y, z),
        )

    sends = []

    def go(copy):
        copy.start()
        sends.append(copy)

    def arrived(f, row):
        remote(
            cots.at[f, row], cots.at[f, row], own_send.at[0, 0], cot_sem.at[f, row], sister
        ).wait_recv()

    def blocks_to(n, src, core, dy):
        return remote(
            src, act_all.at[pl.ds(lead + PER * core, PER), y], a_snd.at[n], a_rcv.at[n],
            dev(x, c, (y + dy) % Y, z),
        )

    for d in range(1, Z):
        @pl.when(z >= d)
        def _():
            pl.semaphore_signal(
                z_ready, inc=1, device_id=dev(x, c, y, (z + Z - d) % Z), device_id_type=MESH
            )

    mine = (z % CORES) == c
    wsrc = weight.at[:, y]

    def weight_to(d):
        return remote(
            wsrc, w_all.at[:, z // CORES], w_snd.at[d - 1], w_rcv.at[z // CORES],
            dev(x, c, y, (z + d) % Z),
        )

    @pl.when(mine)
    def _():
        pltpu.make_async_copy(wsrc, w_all.at[:, z // CORES], w_rcv.at[z // CORES]).start()
        for d in range(1, Z):
            @pl.when(z + d >= Z)
            def _():
                weight_to(d).start()

    go(remote(
        act_send.at[pl.ds((1 - c) * Y, Y)], act_mid, a_snd.at[0], a_rcv.at[0], sister
    ))
    for k in range(PER):
        go(cot_to(k, None, sister, sis_send.at[k, 0]))
    for dy in range(1, Y):
        go(blocks_to(dy, act_send.at[c * Y + (y + dy) % Y], c, dy))
    act_all[pl.ds(lead + PER * c, PER), y] = act_send[c * Y + y]
    mid = remote(act_mid, act_mid, a_snd.at[0], a_rcv.at[0], sister)
    mid.wait_recv()
    for dy in range(1, Y):
        go(blocks_to(Y - 1 + dy, act_mid.at[(y + dy) % Y], 1 - c, dy))
    for k in range(PER):
        ends = (up, down) if k == 0 else (down, up)
        for n, row in enumerate(ends):
            go(cot_to(k, None, dev(x, c, row, z), own_send.at[k, n]))
    act_all[pl.ds(lead + PER * (1 - c), PER), y] = act_mid[y]

    def clear(s, _):
        grad[s] = jnp.zeros(grad.shape[1:], F32)
        return 0

    def clear_edges(s, _):
        for edge in (0, Y + 1):
            lhs[s, edge] = jnp.zeros(lhs.shape[2:], BF16)
        return 0

    lax.fori_loop(0, span, clear, 0)
    lax.fori_loop(0, span + lead, clear_edges, 0)
    total[...] = jnp.zeros(total.shape, F32)

    for k in range(PER):
        arrived(PER * c + k, y)

    def halo_late(row, slot):
        @pl.when(c == 1)
        def _():
            arrived(1, row)
            halo_to(row, slot).start()

    @pl.when(c == 0)
    def _():
        halo_to(y, 0).start()

    halo_late(y, 0)
    for dy in range(1, Y):
        for n, core in ((dy, c), (Y - 1 + dy, 1 - c)):
            blocks = act_all.at[pl.ds(lead + PER * core, PER), (y + Y - dy) % Y]
            remote(blocks, blocks, a_snd.at[n], a_rcv.at[n], sister).wait_recv()
    go(remote(
        act_all.at[pl.ds(span, lead)], act_all.at[pl.ds(0, lead)], p_snd, p_rcv, dev(next_x, c, y, z)
    ))

    i = lax.broadcasted_iota(jnp.int32, (chunk, 1), 0)
    channel = (i // Z) * half + c * per_core + y * Z + i % Z
    groups = centre.shape[1]
    group = (i // Z) * (groups // X) + c * (groups // X // CORES) + y

    def column(row, index):
        lane = lax.broadcasted_iota(jnp.int32, (chunk, row.shape[1]), 1)
        return jnp.sum(jnp.where(lane == index, row, 0.0), axis=1, keepdims=True)

    mean, scale = column(centre[...], group), column(spread[...], group)
    gains, biases = column(gain[...], channel), column(bias[...], channel)
    clip_len = clip_frames[0]

    def valid(f):
        t = x * span + f
        return jnp.where((t >= 0) & (t < clip_len), 1.0, 0.0).astype(F32)

    lane = lax.broadcasted_iota(jnp.int32, (chunk, cols), 1)

    def block_input(s, r):
        norm = (act_all[s + lead, r].astype(F32) - mean) * scale
        shifted = norm * gains + biases
        sig = jax.nn.sigmoid(shifted)
        a = shifted * sig * valid(s)
        at = s + lead
        lhs[at, r + 1, pl.ds(0, chunk)] = jnp.where(lane == 0, 0.0, pltpu.roll(a, 1, 1)).astype(BF16)
        lhs[at, r + 1, pl.ds(chunk, chunk)] = a.astype(BF16)
        lhs[at, r + 1, pl.ds(2 * chunk, chunk)] = jnp.where(
            lane == cols - 1, 0.0, pltpu.roll(a, cols - 1, 1)
        ).astype(BF16)
        return norm, shifted, sig

    def prepare(t, _):
        s, r = t // Y, t % Y
        norm, shifted, sig = block_input(s, r)
        normed[s, r] = norm
        slope[s, r] = sig * (1.0 + shifted * (1.0 - sig)) * valid(s) * gains
        return 0

    def prepare_before(t, _):
        block_input(t // Y - lead, t % Y)
        return 0

    lax.fori_loop(0, span * Y, prepare, 0, unroll=4)

    rows3 = lhs.shape[2]

    def masked(f, r):
        return jnp.where(x * span + f < clip_len, cots[f, r], jnp.zeros((cols, ch), BF16))

    def weight_row(r):
        for f in range(span):
            @pl.when((c != f // PER) & ((c == 0) | (f != 1)))
            def _():
                arrived(f, r)

        left = [lhs[pl.ds(f, 3), pl.ds(r, 3)].reshape(9 * rows3, cols) for f in range(span)]
        right = [masked(f, r) for f in range(span)]
        term = nn(jnp.concatenate(left, axis=1), jnp.concatenate(right, axis=0))
        total[...] += term.reshape(27, chunk, ch)

    parts = [(t, min(8, 27 - t)) for t in range(0, 27, 8)]

    def sent_rows(taps):
        return -(-taps * Z // 16) * 16

    def reduce_x(j):
        tap, taps = parts[j]
        rows, whole = taps * Z, sent_rows(taps)
        for xx in range(X):
            x_send[j, xx, pl.ds(0, rows)] = (
                total[pl.ds(tap, taps), pl.ds(xx * Z, Z)].reshape(rows, ch).astype(BF16)
            )
            if whole > rows:
                x_send[j, xx, pl.ds(rows, whole - rows)] = jnp.zeros((whole - rows, ch), BF16)
        for d in range(1, X):
            xx = (x + d) % X
            go(remote(
                x_send.at[j, xx, pl.ds(0, whole)], x_recv.at[j, d - 1, pl.ds(0, whole)],
                x_snd.at[j, d - 1], x_rcv.at[j, d - 1], dev(xx, c, y, z),
            ))

    def reduce_z(j):
        tap, taps = parts[j]
        rows, whole = taps * Z, sent_rows(taps)
        for d in range(1, X):
            got = x_recv.at[j, d - 1, pl.ds(0, whole)]
            pltpu.make_async_copy(got, got, x_rcv.at[j, d - 1]).wait()
        part = total[pl.ds(tap, taps), pl.ds(x * Z, Z)].reshape(rows, ch)
        for d in range(1, X):
            part = part + x_recv[j, d - 1, pl.ds(0, rows)].astype(F32)
        for h in range(halves):
            row_sum[h, pl.ds(0, rows)] = part[:, h * 128 : (h + 1) * 128]
        for zz in range(Z):
            for h in range(halves):
                z_send[j, zz, :, pl.ds(h * 128, 128)] = row_sum[h, pl.ds(zz, 8, Z), :]
        for d in range(1, Z):
            zz = (z + d) % Z
            go(remote(
                z_send.at[j, zz], z_recv.at[j, d - 1], z_snd.at[j, d - 1], z_rcv.at[j, d - 1],
                dev(x, c, y, zz),
            ))


    across = (y + 2) % Y
    seen = [1, 1]

    def take(k, row, on):
        arrived(PER * c + k, row)
        if on is not None:
            go(cot_to(k, row, dev(x, c, on, z), fwd_send.at[k]))
        n = seen[k]
        seen[k] += 1
        go(cot_to(k, row, sister, sis_send.at[k, n]))

        if k == 0:
            @pl.when(c == 0)
            def _():
                halo_to(row, n).start()

    take(0, down, up)
    take(0, up, None)

    @pl.when(z < Z - 1)
    def _():
        pl.semaphore_wait(z_ready, Z - 1 - z)

    @pl.when(mine)
    def _():
        for d in range(1, Z):
            @pl.when(z + d < Z)
            def _():
                weight_to(d).start()

    pltpu.make_async_copy(act_all.at[pl.ds(0, lead)], act_all.at[pl.ds(0, lead)], p_rcv).wait()
    lax.fori_loop(0, lead * Y, prepare_before, 0, unroll=2)
    take(1, up, down)
    take(1, down, None)
    halo_late(down, 1)
    halo_late(up, 2)

    def turn(n):
        return (y + n + (n // 2) * (1 - 2 * (n % 2))) % Y

    def early(n, _):
        weight_row(turn(n))
        return 0

    lax.fori_loop(0, Y - 1, early, 0)

    def halo_on(d):
        r = (y + d) % Y
        arrived(span + c, r)
        go(remote(
            cots.at[span + c, r], cots.at[span + c, r], fwd_send.at[PER + d], cot_sem.at[span + c, r],
            sister,
        ))

    halo_on(0)
    take(0, across, None)
    take(1, across, None)
    halo_late(across, 3)
    weight_row(across)
    row_sum[...] = jnp.zeros(row_sum.shape, F32)
    for j in range(len(parts)):
        reduce_x(j)

    for n in range(X):
        pltpu.make_async_copy(w_all.at[:, n], w_all.at[:, n], w_rcv.at[n]).wait()

    for k in range(9):
        tap = w_all[pl.ds(3 * k, 3)].astype(F32).reshape(rows3, ch)
        w_taps[pl.ds(k % 3 * rows3, rows3), pl.ds((2 - k // 3) * ch, ch)] = tap.astype(BF16)

    def input_term(s, f0, f1, r):
        k0, k1 = (f0 - s) * ch, (f1 - s) * ch
        right = jnp.concatenate([masked(f, r) for f in range(f0, f1)], axis=1)
        part = nt(w_taps[:, pl.ds(k0, k1 - k0)], right)
        grad[s, pl.ds(r, 3)] += part.reshape(3, rows3, cols)

    def input_rows(n, _):
        for s in range(span):
            input_term(s, s, min(s + 3, span), turn(n))
        return 0

    def halo_input(d):
        r = (y + d) % Y
        for f in range(span, span + lead):
            @pl.when(c != f - span)
            def _():
                arrived(f, r)

        for s in range(span - lead, span):
            input_term(s, span, s + 3, r)

    lax.fori_loop(0, 2, input_rows, 0)
    halo_on(1)
    halo_on(3)
    lax.fori_loop(2, Y, input_rows, 0)

    def gather(t, carry):
        first, second = carry
        s, r = t // Y, t % Y
        g0 = grad[s, r + 1, pl.ds(0, chunk)]
        g1 = grad[s, r + 1, pl.ds(chunk, chunk)]
        g2 = grad[s, r + 1, pl.ds(2 * chunk, chunk)]
        whole = (
            jnp.where(lane == cols - 1, 0.0, pltpu.roll(g0, cols - 1, 1)) + g1
            + jnp.where(lane == 0, 0.0, pltpu.roll(g2, 1, 1))
        )
        upstream = whole * slope[s, r]
        slope[s, r] = upstream
        return first + upstream, second + upstream * normed[s, r]

    nothing = jnp.zeros((chunk, cols), F32)
    early_sums = lax.fori_loop(0, (span - lead) * Y, gather, (nothing, nothing), unroll=4)
    for d in (0, 1, 3):
        halo_input(d)
    reduce_z(0)
    halo_on(2)
    reduce_z(1)
    halo_input(2)
    first, second = lax.fori_loop((span - lead) * Y, span * Y, gather, early_sums, unroll=8)
    slim = lax.broadcasted_iota(jnp.int32, (chunk, 128), 1)
    first = jnp.sum(first, axis=1, keepdims=True)
    second = jnp.sum(second, axis=1, keepdims=True)
    s_send[...] = jnp.where(slim == 0, first, jnp.where(slim == 1, second, 0.0))
    for d in range(1, X):
        go(remote(
            s_send, s_recv.at[d - 1], s_snd.at[d - 1], s_rcv.at[d - 1], dev((x + d) % X, c, y, z)
        ))

    reduce_z(2)
    reduce_z(3)

    for d in range(1, X):
        pltpu.make_async_copy(s_recv.at[d - 1], s_recv.at[d - 1], s_rcv.at[d - 1]).wait()
    both = s_send[...]
    for d in range(1, X):
        both = both + s_recv[d - 1]
    both = both.reshape(X, Z, 128)
    both = jnp.broadcast_to(jnp.sum(both, axis=1, keepdims=True), (X, Z, 128)).reshape(chunk, 128)
    population = clip_len.astype(F32) * (Y * cols * Z)
    first = jnp.sum(jnp.where(slim == 0, both, 0.0), axis=1, keepdims=True) / population
    second = jnp.sum(jnp.where(slim == 1, both, 0.0), axis=1, keepdims=True) / population

    def finish(core):
        def body(t, _):
            s, r = PER * core + t // Y, t % Y
            value = scale * (slope[s, r] - first - normed[s, r] * second) * valid(s)
            g_send[s, r] = value.astype(BF16)
            return 0

        lax.fori_loop(0, PER * Y, body, 0, unroll=8)

    def rows_to(n, src, core, dy):
        return remote(
            src, g_recv.at[core * Y + y], g_snd.at[n], g_rcv.at[n], dev(x, c, (y + dy) % Y, z)
        )

    finish(c)
    for dy in range(1, Y):
        go(rows_to(dy, g_send.at[pl.ds(PER * c, PER), (y + dy) % Y], c, dy))
    finish(1 - c)
    go(remote(g_send.at[pl.ds(PER * (1 - c), PER)], g_mid, g_snd.at[0], g_rcv.at[0], sister))
    g_recv[c * Y + y] = g_send[pl.ds(PER * c, PER), y]
    remote(g_mid, g_mid, g_snd.at[0], g_rcv.at[0], sister).wait_recv()
    for dy in range(1, Y):
        go(rows_to(Y - 1 + dy, g_mid.at[:, (y + dy) % Y], 1 - c, dy))
    g_recv[(1 - c) * Y + y] = g_mid[:, y]

    final = z_send[:, z]
    for j in range(len(parts)):
        for d in range(1, Z):
            pltpu.make_async_copy(z_recv.at[j, d - 1], z_recv.at[j, d - 1], z_rcv.at[j, d - 1]).wait()
    for d in range(1, Z):
        final = final + z_recv[:, d - 1]
    final = final.reshape(len(parts) * 8, ch)[:27]
    cells = X * Y * Z * CORES * PER * cols
    wout[...] = (final * (1.0 / cells)).astype(BF16)

    for dy in range(1, Y):
        for n, core in ((dy, c), (Y - 1 + dy, 1 - c)):
            rows = g_recv.at[core * Y + (y + Y - dy) % Y]
            remote(rows, rows, g_snd.at[n], g_rcv.at[n], sister).wait_recv()
    for k in range(PER):
        out[k] = tn(g_recv[:, k].reshape(ch, cols), pick).astype(BF16)

    for copy in sends:
        copy.wait_send()

    for n in range(Y):
        halo_to(y, n).wait_send()

    @pl.when(mine)
    def _():
        for d in range(1, Z):
            weight_to(d).wait_send()


def per_device(X, Y, Z, acts, cot, clip_frames, weight, centre, spread, gain, bias):
    _, per, _, cols, ch = acts.shape
    span, lead = CORES * per, 2
    chunk = ch // (CORES * Y)
    taps = weight.shape[1]
    dma = pltpu.SemaphoreType.DMA
    hbm = pl.BlockSpec(memory_space=pl.ANY)
    vmem = pl.BlockSpec(memory_space=pltpu.VMEM)
    grad_input, weight_grad = pl.pallas_call(
        functools.partial(fused, X, Y, Z),
        out_shape=(
            jax.ShapeDtypeStruct((per, cols, ch), BF16),
            jax.ShapeDtypeStruct((taps, ch), BF16),
        ),
        in_specs=[pl.BlockSpec(memory_space=pltpu.SMEM), hbm, hbm, hbm, vmem, vmem, vmem, vmem],
        out_specs=(vmem, vmem),
        scratch_shapes=[
            pltpu.VMEM((per, cols, ch), BF16),
            pltpu.VMEM((CORES * Y, per, chunk, cols), BF16),
            pltpu.VMEM((Y, per, chunk, cols), BF16),
            pltpu.VMEM((span + lead, Y, chunk, cols), BF16),
            pltpu.VMEM((span + lead, Y, cols, ch), BF16),
            pltpu.VMEM((taps, X, Z, ch), BF16),
            pltpu.VMEM((9 * chunk, 3 * ch), BF16),
            pltpu.VMEM((span + lead, Y + 2, 3 * chunk, cols), BF16),
            pltpu.VMEM((span, Y + 2, 3 * chunk, cols), F32),
            pltpu.VMEM((span, Y, chunk, cols), F32),
            pltpu.VMEM((span, Y, chunk, cols), F32),
            pltpu.VMEM((taps, chunk, ch), F32),
            pltpu.VMEM((4, X, 8 * Z, ch), BF16),
            pltpu.VMEM((4, X - 1, 8 * Z, ch), BF16),
            pltpu.VMEM((ch // 128, 8 * Z, 128), F32),
            pltpu.VMEM((4, Z, 8, ch), F32),
            pltpu.VMEM((4, Z - 1, 8, ch), F32),
            pltpu.VMEM((chunk, 128), F32),
            pltpu.VMEM((X - 1, chunk, 128), F32),
            pltpu.VMEM((span, Y, chunk, cols), BF16),
            pltpu.VMEM((per, Y, chunk, cols), BF16),
            pltpu.VMEM((CORES * Y, per, chunk, cols), BF16),
            dma,
            dma((span + lead, Y)),
            dma((per, 2)),
            dma((per + Y,)),
            dma((per, Y)),
            dma((Y,)),
            dma((CORES * Y - 1,)),
            dma((CORES * Y - 1,)),
            dma((Z - 1,)),
            dma((X,)),
            dma((4, X - 1)),
            dma((4, X - 1)),
            dma((4, Z - 1)),
            dma((4, Z - 1)),
            dma((X - 1,)),
            dma((X - 1,)),
            dma((CORES * Y - 1,)),
            dma((CORES * Y - 1,)),
            dma,
            dma,
            pltpu.SemaphoreType.REGULAR,
        ],
        compiler_params=pltpu.CompilerParams(
            collective_id=0, has_side_effects=True, vmem_limit_bytes=54784 * 1024
        ),
    )(
        clip_frames,
        acts.reshape(per, cols, ch),
        cot.reshape(per, cols, ch),
        weight.transpose(1, 0, 2).reshape(taps, Y, Z, ch),
        centre,
        spread,
        gain.reshape(1, ch),
        bias.reshape(1, ch),
    )
    return grad_input.reshape(1, per, 1, cols, ch), weight_grad


def solution(mesh):
    X, Y, Z = mesh.shape["tm"] // CORES, mesh.shape["height"], mesh.shape["dp"]
    return jax.shard_map(
        functools.partial(per_device, X, Y, Z),
        mesh=mesh,
        in_specs=(
            P("dp", "tm", "height", None, None),
            P("dp", "tm", "height", None, None),
            P("dp"),
            P("dp", None, None),
            P("dp", None),
            P("dp", None),
            P(),
            P(),
        ),
        out_specs=(P("dp", "tm", "height", None, None), P(("tm", "height", "dp"), None)),
        check_vma=False,
    )
```

```python
import functools

import jax
import jax.numpy as jnp
from jax import lax
from jax.experimental import pallas as pl
from jax.experimental.pallas import tpu as pltpu
from jax.sharding import PartitionSpec as P

CORES = 2
PER = 2
MESH = pl.DeviceIdType.MESH
F32 = jnp.float32
BF16 = jnp.bfloat16


def nt(a, b):
    return lax.dot_general(a, b, (((1,), (1,)), ((), ())), preferred_element_type=F32)


def nn(a, b):
    return lax.dot_general(a, b, (((1,), (0,)), ((), ())), preferred_element_type=F32)


def tn(a, b):
    return lax.dot_general(a, b, (((0,), (0,)), ((), ())), preferred_element_type=F32)


def fused(
    X, Y, Z,
    clip_frames, acts, cot, weight, centre, spread, gain, bias,
    out, wout,
    act_in, act_send, act_mid, act_all, cots, w_all, w_taps, lhs, grad, normed, slope,
    total, x_send, x_recv, row_sum, z_send, z_recv, s_send, s_recv, g_send, g_mid, g_recv,
    act_sem, cot_sem, own_send, fwd_send, sis_send, halo_send, a_snd, a_rcv, w_snd, w_rcv,
    x_snd, x_rcv, z_snd, z_rcv, s_snd, s_rcv, g_snd, g_rcv, p_snd, p_rcv, z_ready,
):
    tm = lax.axis_index("tm")
    y = lax.axis_index("height")
    z = lax.axis_index("dp")
    x = tm // CORES
    c = tm % CORES
    span = CORES * PER
    cols, ch = cots.shape[2], cots.shape[3]
    chunk = act_all.shape[2]
    lead = 2
    halves = ch // 128

    def dev(xx, cc, yy, zz):
        return (xx * CORES + cc, yy, zz)

    def remote(src, dst, snd, rcv, target):
        return pltpu.make_async_remote_copy(
            src_ref=src, dst_ref=dst, send_sem=snd, recv_sem=rcv,
            device_id=target, device_id_type=MESH,
        )

    up, down = (y + 1) % Y, (y + Y - 1) % Y
    prev_x, next_x = (x + X - 1) % X, (x + 1) % X
    sister = dev(x, 1 - c, y, z)

    act_copy = pltpu.make_async_copy(acts, act_in, act_sem)
    act_copy.start()
    for k in range(PER):
        pltpu.make_async_copy(cot.at[k], cots.at[PER * c + k, y], cot_sem.at[PER * c + k, y]).start()

    barrier = pltpu.get_barrier_semaphore()
    partners = [sister] + [dev(x, c, (y + dy) % Y, z) for dy in range(1, Y)]
    partners += [dev((x + dx) % X, c, y, z) for dx in range(1, X)]
    for target in partners:
        pl.semaphore_signal(barrier, inc=1, device_id=target, device_id_type=MESH)

    for d in range(1, Z):
        @pl.when(z + d < Z)
        def _():
            pl.semaphore_signal(
                barrier, inc=1, device_id=dev(x, c, y, (z + d) % Z), device_id_type=MESH
            )

    row_id = lax.broadcasted_iota(jnp.int32, (ch, ch), 0)
    col_id = lax.broadcasted_iota(jnp.int32, (ch, ch), 1)
    half = ch // X
    per_core = half // CORES
    order = (
        ((row_id // Z) % X) * half + (row_id // (chunk * Y)) * per_core
        + ((row_id // chunk) % Y) * Z + row_id % Z
    )
    pick = jnp.where(order == col_id, 1.0, 0.0).astype(BF16)
    act_copy.wait()
    for k in range(PER):
        act_send[:, k] = nt(pick, act_in[k]).astype(BF16).reshape(CORES * Y, chunk, cols)

    pl.semaphore_wait(barrier, len(partners) + z)

    def cot_to(k, row, target, snd):
        src = cot.at[k] if row is None else cots.at[PER * c + k, row]
        at = y if row is None else row
        return remote(src, cots.at[PER * c + k, at], snd, cot_sem.at[PER * c + k, at], target)

    def halo_to(row, slot):
        return remote(
            cots.at[c, row], cots.at[span + c, row], halo_send.at[slot], cot_sem.at[span + c, row],
            dev(prev_x, c, y, z),
        )

    sends = []

    def go(copy):
        copy.start()
        sends.append(copy)

    def arrived(f, row):
        remote(
            cots.at[f, row], cots.at[f, row], own_send.at[0, 0], cot_sem.at[f, row], sister
        ).wait_recv()

    def blocks_to(n, src, core, dy):
        return remote(
            src, act_all.at[pl.ds(lead + PER * core, PER), y], a_snd.at[n], a_rcv.at[n],
            dev(x, c, (y + dy) % Y, z),
        )

    for d in range(1, Z):
        @pl.when(z >= d)
        def _():
            pl.semaphore_signal(
                z_ready, inc=1, device_id=dev(x, c, y, (z + Z - d) % Z), device_id_type=MESH
            )

    mine = (z % CORES) == c
    wsrc = weight.at[:, y]

    def weight_to(d):
        return remote(
            wsrc, w_all.at[:, z // CORES], w_snd.at[d - 1], w_rcv.at[z // CORES],
            dev(x, c, y, (z + d) % Z),
        )

    @pl.when(mine)
    def _():
        pltpu.make_async_copy(wsrc, w_all.at[:, z // CORES], w_rcv.at[z // CORES]).start()
        for d in range(1, Z):
            @pl.when(z + d >= Z)
            def _():
                weight_to(d).start()

    go(remote(
        act_send.at[pl.ds((1 - c) * Y, Y)], act_mid, a_snd.at[0], a_rcv.at[0], sister
    ))
    for k in range(PER):
        go(cot_to(k, None, sister, sis_send.at[k, 0]))
    for dy in range(1, Y):
        go(blocks_to(dy, act_send.at[c * Y + (y + dy) % Y], c, dy))
    act_all[pl.ds(lead + PER * c, PER), y] = act_send[c * Y + y]
    mid = remote(act_mid, act_mid, a_snd.at[0], a_rcv.at[0], sister)
    mid.wait_recv()
    for dy in range(1, Y):
        go(blocks_to(Y - 1 + dy, act_mid.at[(y + dy) % Y], 1 - c, dy))
    for k in range(PER):
        ends = (up, down) if k == 0 else (down, up)
        for n, row in enumerate(ends):
            go(cot_to(k, None, dev(x, c, row, z), own_send.at[k, n]))
    act_all[pl.ds(lead + PER * (1 - c), PER), y] = act_mid[y]

    def clear(s, _):
        grad[s] = jnp.zeros(grad.shape[1:], F32)
        return 0

    def clear_edges(s, _):
        for edge in (0, Y + 1):
            lhs[s, edge] = jnp.zeros(lhs.shape[2:], BF16)
        return 0

    lax.fori_loop(0, span, clear, 0)
    lax.fori_loop(0, span + lead, clear_edges, 0)
    total[...] = jnp.zeros(total.shape, F32)

    for k in range(PER):
        arrived(PER * c + k, y)

    def halo_late(row, slot):
        @pl.when(c == 1)
        def _():
            arrived(1, row)
            halo_to(row, slot).start()

    @pl.when(c == 0)
    def _():
        halo_to(y, 0).start()

    halo_late(y, 0)
    for dy in range(1, Y):
        for n, core in ((dy, c), (Y - 1 + dy, 1 - c)):
            blocks = act_all.at[pl.ds(lead + PER * core, PER), (y + Y - dy) % Y]
            remote(blocks, blocks, a_snd.at[n], a_rcv.at[n], sister).wait_recv()
    go(remote(
        act_all.at[pl.ds(span, lead)], act_all.at[pl.ds(0, lead)], p_snd, p_rcv, dev(next_x, c, y, z)
    ))

    i = lax.broadcasted_iota(jnp.int32, (chunk, 1), 0)
    channel = (i // Z) * half + c * per_core + y * Z + i % Z
    groups = centre.shape[1]
    group = (i // Z) * (groups // X) + c * (groups // X // CORES) + y

    def column(row, index):
        lane = lax.broadcasted_iota(jnp.int32, (chunk, row.shape[1]), 1)
        return jnp.sum(jnp.where(lane == index, row, 0.0), axis=1, keepdims=True)

    mean, scale = column(centre[...], group), column(spread[...], group)
    gains, biases = column(gain[...], channel), column(bias[...], channel)
    clip_len = clip_frames[0]

    def valid(f):
        t = x * span + f
        return jnp.where((t >= 0) & (t < clip_len), 1.0, 0.0).astype(F32)

    lane = lax.broadcasted_iota(jnp.int32, (chunk, cols), 1)

    def block_input(s, r):
        norm = (act_all[s + lead, r].astype(F32) - mean) * scale
        shifted = norm * gains + biases
        sig = jax.nn.sigmoid(shifted)
        a = shifted * sig * valid(s)
        at = s + lead
        lhs[at, r + 1, pl.ds(0, chunk)] = jnp.where(lane == 0, 0.0, pltpu.roll(a, 1, 1)).astype(BF16)
        lhs[at, r + 1, pl.ds(chunk, chunk)] = a.astype(BF16)
        lhs[at, r + 1, pl.ds(2 * chunk, chunk)] = jnp.where(
            lane == cols - 1, 0.0, pltpu.roll(a, cols - 1, 1)
        ).astype(BF16)
        return norm, shifted, sig

    def prepare(t, _):
        s, r = t // Y, t % Y
        norm, shifted, sig = block_input(s, r)
        normed[s, r] = norm
        slope[s, r] = sig * (1.0 + shifted * (1.0 - sig)) * valid(s) * gains
        return 0

    def prepare_before(t, _):
        block_input(t // Y - lead, t % Y)
        return 0

    lax.fori_loop(0, span * Y, prepare, 0, unroll=4)

    rows3 = lhs.shape[2]

    def masked(f, r):
        if f < span - 1:
            return cots[f, r]
        return jnp.where(x * span + f < clip_len, cots[f, r], jnp.zeros((cols, ch), BF16))

    def weight_row(r):
        for f in range(span):
            @pl.when((c != f // PER) & ((c == 0) | (f != 1)))
            def _():
                arrived(f, r)

        left = [lhs[pl.ds(f, 3), pl.ds(r, 3)].reshape(9 * rows3, cols) for f in range(span)]
        right = [masked(f, r) for f in range(span)]
        term = nn(jnp.concatenate(left, axis=1), jnp.concatenate(right, axis=0))
        total[...] += term.reshape(27, chunk, ch)

    parts = [(t, min(8, 27 - t)) for t in range(0, 27, 8)]

    def sent_rows(taps):
        return -(-taps * Z // 16) * 16

    def reduce_x(j):
        tap, taps = parts[j]
        rows, whole = taps * Z, sent_rows(taps)
        for xx in range(X):
            x_send[j, xx, pl.ds(0, rows)] = (
                total[pl.ds(tap, taps), pl.ds(xx * Z, Z)].reshape(rows, ch).astype(BF16)
            )
            if whole > rows:
                x_send[j, xx, pl.ds(rows, whole - rows)] = jnp.zeros((whole - rows, ch), BF16)
        for d in range(1, X):
            xx = (x + d) % X
            go(remote(
                x_send.at[j, xx, pl.ds(0, whole)], x_recv.at[j, d - 1, pl.ds(0, whole)],
                x_snd.at[j, d - 1], x_rcv.at[j, d - 1], dev(xx, c, y, z),
            ))

    def reduce_z(j):
        tap, taps = parts[j]
        rows, whole = taps * Z, sent_rows(taps)
        for d in range(1, X):
            got = x_recv.at[j, d - 1, pl.ds(0, whole)]
            pltpu.make_async_copy(got, got, x_rcv.at[j, d - 1]).wait()
        part = total[pl.ds(tap, taps), pl.ds(x * Z, Z)].reshape(rows, ch)
        for d in range(1, X):
            part = part + x_recv[j, d - 1, pl.ds(0, rows)].astype(F32)
        for h in range(halves):
            row_sum[h, pl.ds(0, rows)] = part[:, h * 128 : (h + 1) * 128]
        for zz in range(Z):
            for h in range(halves):
                z_send[j, zz, :, pl.ds(h * 128, 128)] = row_sum[h, pl.ds(zz, 8, Z), :]
        for d in range(1, Z):
            zz = (z + d) % Z
            go(remote(
                z_send.at[j, zz], z_recv.at[j, d - 1], z_snd.at[j, d - 1], z_rcv.at[j, d - 1],
                dev(x, c, y, zz),
            ))


    across = (y + 2) % Y
    seen = [1, 1]

    def take(k, row, on):
        arrived(PER * c + k, row)
        if on is not None:
            go(cot_to(k, row, dev(x, c, on, z), fwd_send.at[k]))
        n = seen[k]
        seen[k] += 1
        go(cot_to(k, row, sister, sis_send.at[k, n]))

        if k == 0:
            @pl.when(c == 0)
            def _():
                halo_to(row, n).start()

    take(0, down, up)
    take(0, up, None)

    @pl.when(z < Z - 1)
    def _():
        pl.semaphore_wait(z_ready, Z - 1 - z)

    @pl.when(mine)
    def _():
        for d in range(1, Z):
            @pl.when(z + d < Z)
            def _():
                weight_to(d).start()

    pltpu.make_async_copy(act_all.at[pl.ds(0, lead)], act_all.at[pl.ds(0, lead)], p_rcv).wait()
    lax.fori_loop(0, lead * Y, prepare_before, 0, unroll=2)
    take(1, up, down)
    take(1, down, None)
    halo_late(down, 1)
    halo_late(up, 2)

    def turn(n):
        return (y + n + (n // 2) * (1 - 2 * (n % 2))) % Y

    def early(n, _):
        weight_row(turn(n))
        return 0

    lax.fori_loop(0, Y - 1, early, 0)

    def halo_on(d):
        r = (y + d) % Y
        arrived(span + c, r)
        go(remote(
            cots.at[span + c, r], cots.at[span + c, r], fwd_send.at[PER + d], cot_sem.at[span + c, r],
            sister,
        ))

    halo_on(0)
    take(0, across, None)
    take(1, across, None)
    halo_late(across, 3)
    weight_row(across)
    row_sum[...] = jnp.zeros(row_sum.shape, F32)
    for j in range(len(parts)):
        reduce_x(j)

    for n in range(X):
        pltpu.make_async_copy(w_all.at[:, n], w_all.at[:, n], w_rcv.at[n]).wait()

    for k in range(9):
        tap = w_all[pl.ds(3 * k, 3)].astype(F32).reshape(rows3, ch)
        w_taps[pl.ds(k % 3 * rows3, rows3), pl.ds((2 - k // 3) * ch, ch)] = tap.astype(BF16)

    def input_term(s, f0, f1, r):
        k0, k1 = (f0 - s) * ch, (f1 - s) * ch
        right = jnp.concatenate([masked(f, r) for f in range(f0, f1)], axis=1)
        part = nt(w_taps[:, pl.ds(k0, k1 - k0)], right)
        grad[s, pl.ds(r, 3)] += part.reshape(3, rows3, cols)

    def input_rows(n, _):
        for s in range(span):
            input_term(s, s, min(s + 3, span), turn(n))
        return 0

    def halo_input(d):
        r = (y + d) % Y
        for f in range(span, span + lead):
            @pl.when(c != f - span)
            def _():
                arrived(f, r)

        for s in range(span - lead, span):
            input_term(s, span, s + 3, r)

    lax.fori_loop(0, 2, input_rows, 0)
    halo_on(1)
    halo_on(3)
    lax.fori_loop(2, Y, input_rows, 0)

    def gather(t, carry):
        first, second = carry
        s, r = t // Y, t % Y
        g0 = grad[s, r + 1, pl.ds(0, chunk)]
        g1 = grad[s, r + 1, pl.ds(chunk, chunk)]
        g2 = grad[s, r + 1, pl.ds(2 * chunk, chunk)]
        whole = (
            jnp.where(lane == cols - 1, 0.0, pltpu.roll(g0, cols - 1, 1)) + g1
            + jnp.where(lane == 0, 0.0, pltpu.roll(g2, 1, 1))
        )
        upstream = whole * slope[s, r]
        slope[s, r] = upstream
        return first + upstream, second + upstream * normed[s, r]

    nothing = jnp.zeros((chunk, cols), F32)
    early_sums = lax.fori_loop(0, (span - lead) * Y, gather, (nothing, nothing), unroll=4)
    for d in (0, 1, 3):
        halo_input(d)
    reduce_z(0)
    halo_on(2)
    reduce_z(1)
    halo_input(2)
    first, second = lax.fori_loop((span - lead) * Y, span * Y, gather, early_sums, unroll=8)
    slim = lax.broadcasted_iota(jnp.int32, (chunk, 128), 1)
    first = jnp.sum(first, axis=1, keepdims=True)
    second = jnp.sum(second, axis=1, keepdims=True)
    s_send[...] = jnp.where(slim == 0, first, jnp.where(slim == 1, second, 0.0))
    for d in range(1, X):
        go(remote(
            s_send, s_recv.at[d - 1], s_snd.at[d - 1], s_rcv.at[d - 1], dev((x + d) % X, c, y, z)
        ))

    reduce_z(2)
    reduce_z(3)

    for d in range(1, X):
        pltpu.make_async_copy(s_recv.at[d - 1], s_recv.at[d - 1], s_rcv.at[d - 1]).wait()
    both = s_send[...]
    for d in range(1, X):
        both = both + s_recv[d - 1]
    both = both.reshape(X, Z, 128)
    both = jnp.broadcast_to(jnp.sum(both, axis=1, keepdims=True), (X, Z, 128)).reshape(chunk, 128)
    population = clip_len.astype(F32) * (Y * cols * Z)
    first = jnp.sum(jnp.where(slim == 0, both, 0.0), axis=1, keepdims=True) / population
    second = jnp.sum(jnp.where(slim == 1, both, 0.0), axis=1, keepdims=True) / population

    def finish(core):
        def body(t, _):
            s, r = PER * core + t // Y, t % Y
            value = scale * (slope[s, r] - first - normed[s, r] * second) * valid(s)
            g_send[s, r] = value.astype(BF16)
            return 0

        lax.fori_loop(0, PER * Y, body, 0, unroll=8)

    def rows_to(n, src, core, dy):
        return remote(
            src, g_recv.at[core * Y + y], g_snd.at[n], g_rcv.at[n], dev(x, c, (y + dy) % Y, z)
        )

    finish(c)
    for dy in range(1, Y):
        go(rows_to(dy, g_send.at[pl.ds(PER * c, PER), (y + dy) % Y], c, dy))
    finish(1 - c)
    go(remote(g_send.at[pl.ds(PER * (1 - c), PER)], g_mid, g_snd.at[0], g_rcv.at[0], sister))
    g_recv[c * Y + y] = g_send[pl.ds(PER * c, PER), y]
    remote(g_mid, g_mid, g_snd.at[0], g_rcv.at[0], sister).wait_recv()
    for dy in range(1, Y):
        go(rows_to(Y - 1 + dy, g_mid.at[:, (y + dy) % Y], 1 - c, dy))
    g_recv[(1 - c) * Y + y] = g_mid[:, y]

    final = z_send[:, z]
    for j in range(len(parts)):
        for d in range(1, Z):
            pltpu.make_async_copy(z_recv.at[j, d - 1], z_recv.at[j, d - 1], z_rcv.at[j, d - 1]).wait()
    for d in range(1, Z):
        final = final + z_recv[:, d - 1]
    final = final.reshape(len(parts) * 8, ch)[:27]
    cells = X * Y * Z * CORES * PER * cols
    wout[...] = (final * (1.0 / cells)).astype(BF16)

    for dy in range(1, Y):
        for n, core in ((dy, c), (Y - 1 + dy, 1 - c)):
            rows = g_recv.at[core * Y + (y + Y - dy) % Y]
            remote(rows, rows, g_snd.at[n], g_rcv.at[n], sister).wait_recv()
    for k in range(PER):
        out[k] = tn(g_recv[:, k].reshape(ch, cols), pick).astype(BF16)

    for copy in sends:
        copy.wait_send()

    for n in range(Y):
        halo_to(y, n).wait_send()

    @pl.when(mine)
    def _():
        for d in range(1, Z):
            weight_to(d).wait_send()


def per_device(X, Y, Z, acts, cot, clip_frames, weight, centre, spread, gain, bias):
    _, per, _, cols, ch = acts.shape
    span, lead = CORES * per, 2
    chunk = ch // (CORES * Y)
    taps = weight.shape[1]
    dma = pltpu.SemaphoreType.DMA
    hbm = pl.BlockSpec(memory_space=pl.ANY)
    vmem = pl.BlockSpec(memory_space=pltpu.VMEM)
    grad_input, weight_grad = pl.pallas_call(
        functools.partial(fused, X, Y, Z),
        out_shape=(
            jax.ShapeDtypeStruct((per, cols, ch), BF16),
            jax.ShapeDtypeStruct((taps, ch), BF16),
        ),
        in_specs=[pl.BlockSpec(memory_space=pltpu.SMEM), hbm, hbm, hbm, vmem, vmem, vmem, vmem],
        out_specs=(vmem, vmem),
        scratch_shapes=[
            pltpu.VMEM((per, cols, ch), BF16),
            pltpu.VMEM((CORES * Y, per, chunk, cols), BF16),
            pltpu.VMEM((Y, per, chunk, cols), BF16),
            pltpu.VMEM((span + lead, Y, chunk, cols), BF16),
            pltpu.VMEM((span + lead, Y, cols, ch), BF16),
            pltpu.VMEM((taps, X, Z, ch), BF16),
            pltpu.VMEM((9 * chunk, 3 * ch), BF16),
            pltpu.VMEM((span + lead, Y + 2, 3 * chunk, cols), BF16),
            pltpu.VMEM((span, Y + 2, 3 * chunk, cols), F32),
            pltpu.VMEM((span, Y, chunk, cols), F32),
            pltpu.VMEM((span, Y, chunk, cols), F32),
            pltpu.VMEM((taps, chunk, ch), F32),
            pltpu.VMEM((4, X, 8 * Z, ch), BF16),
            pltpu.VMEM((4, X - 1, 8 * Z, ch), BF16),
            pltpu.VMEM((ch // 128, 8 * Z, 128), F32),
            pltpu.VMEM((4, Z, 8, ch), F32),
            pltpu.VMEM((4, Z - 1, 8, ch), F32),
            pltpu.VMEM((chunk, 128), F32),
            pltpu.VMEM((X - 1, chunk, 128), F32),
            pltpu.VMEM((span, Y, chunk, cols), BF16),
            pltpu.VMEM((per, Y, chunk, cols), BF16),
            pltpu.VMEM((CORES * Y, per, chunk, cols), BF16),
            dma,
            dma((span + lead, Y)),
            dma((per, 2)),
            dma((per + Y,)),
            dma((per, Y)),
            dma((Y,)),
            dma((CORES * Y - 1,)),
            dma((CORES * Y - 1,)),
            dma((Z - 1,)),
            dma((X,)),
            dma((4, X - 1)),
            dma((4, X - 1)),
            dma((4, Z - 1)),
            dma((4, Z - 1)),
            dma((X - 1,)),
            dma((X - 1,)),
            dma((CORES * Y - 1,)),
            dma((CORES * Y - 1,)),
            dma,
            dma,
            pltpu.SemaphoreType.REGULAR,
        ],
        compiler_params=pltpu.CompilerParams(
            collective_id=0, has_side_effects=True, vmem_limit_bytes=54784 * 1024
        ),
    )(
        clip_frames,
        acts.reshape(per, cols, ch),
        cot.reshape(per, cols, ch),
        weight.transpose(1, 0, 2).reshape(taps, Y, Z, ch),
        centre,
        spread,
        gain.reshape(1, ch),
        bias.reshape(1, ch),
    )
    return grad_input.reshape(1, per, 1, cols, ch), weight_grad


def solution(mesh):
    X, Y, Z = mesh.shape["tm"] // CORES, mesh.shape["height"], mesh.shape["dp"]
    return jax.shard_map(
        functools.partial(per_device, X, Y, Z),
        mesh=mesh,
        in_specs=(
            P("dp", "tm", "height", None, None),
            P("dp", "tm", "height", None, None),
            P("dp"),
            P("dp", None, None),
            P("dp", None),
            P("dp", None),
            P(),
            P(),
        ),
        out_specs=(P("dp", "tm", "height", None, None), P(("tm", "height", "dp"), None)),
        check_vma=False,
    )
```
